32 devices in a mesh: wide: 8 (over y, x, core), narrow: 4 (over z).
Axes of the slice: x: 2, y: 2, z: 4, core: 2. Of those that a mesh axis runs over, the one named last changes fastest.
Arguments:
- amplitudes: bfloat16 [48, 2, 1536, 1536], P('narrow', None, 'wide'), may hold values from -6 to 6
- pair_integrals: bfloat16 [48, 2, 1536, 1536], P('narrow', None, 'wide'), may hold values from -4 to 4
- cycle_integrals: bfloat16 [2, 1536, 2, 1536], P(None, None, None, 'narrow'), may hold values from -0.109375 to 0.109375
- ladder_integrals: bfloat16 [4, 4, 1536, 1536], P(None, None, 'wide', 'narrow'), may hold values from -0.078125 to 0.078125
- occ_energy: float32 [300], replicated, may hold values from -2 to -0.5
- virt_energy: float32 [1536], replicated, may hold values from 0.3 to 3
- occ_irrep: int32 [300], replicated, may hold values from 0 to 1
- virt_irrep: int32 [96], replicated, may hold values from 0 to 1
- slab_i: int32 [48], P('narrow'), may hold values from 0 to 299
- slab_j: int32 [2], replicated, may hold values from 0 to 299
Outputs:
- new_amplitudes: bfloat16 [48, 2, 1536, 1536], P('narrow', None, 'wide')
The draws below stay inside these ranges and needn't reach their ends.
Inputs may be any that keep to these rules, and one draw needn't show every extreme that they name: `slab_i`: each entry names an occupied orbital. `slab_j`: each entry names an occupied orbital.
All inputs are finite; a program needn't handle non-finite values.
Results may differ from the reference program's by a relative error of at most 0.0046.
Values may be sent and summed in bfloat16 or wider, within the bound.
No kernel may reach another device: no remote copies, remote signals or barrier semaphores. Data moves between devices by JAX's collectives and lax.ppermute only.
A program may use at most 192 MiB of HBM per device.

```python
import jax
import jax.numpy as jnp
from jax import lax

NV = 1536
NOCC = 300
NJ = 2
NI = 48
TILE = 4
VBLK = 16


def plant(values, rng, least, top_value):
    index_at = [jax.random.randint(jax.random.fold_in(rng, axis), (), 0, length) for axis, length in enumerate(values.shape)]
    longest = values.shape.index(max(values.shape))
    neighbour = index_at[:longest] + [(index_at[longest] + 1) % values.shape[longest]] + index_at[longest + 1:]
    return values.at[tuple(index_at)].set(least).at[tuple(neighbour)].set(top_value)


def levels(key, dims, split, smallest, top_value):
    loudness = 1.0
    for axis_at, blocks in split:
        heights = jax.random.uniform(jax.random.fold_in(jax.random.fold_in(key, 6), axis_at), (blocks,), jnp.float32, smallest / len(split), top_value / len(split))
        loudness = loudness * jnp.repeat(jnp.exp(heights), dims[axis_at] // blocks).reshape((-1,) + (1,) * (len(dims) - 1 - axis_at))
    return loudness


def noise(key, dims, deviation, most, pieces=(), kind=jnp.bfloat16):
    values = jax.random.normal(key, dims, jnp.float32) * deviation
    if len(pieces) > 0:
        values = levels(key, dims, pieces, -0.22, 0.18) * values
    return jnp.clip(values, min=-most, max=most).astype(kind)


def setup_inputs(seed: int = 0) -> dict:
    keys = jax.random.split(jax.random.key(seed), 11)
    return {
        "amplitudes": noise(keys[0], (NI, NJ, NV, NV), 1.0, 6.0, ((0, 4), (2, 8))),
        "pair_integrals": noise(keys[1], (NI, NJ, NV, NV), 0.5, 4.0, ((0, 4), (2, 8))),
        "cycle_integrals": noise(keys[2], (NJ, NV, NJ, NV), (NJ * NV) ** -0.5, 0.109375, ((3, 4),)),
        "ladder_integrals": noise(keys[3], (TILE, TILE, NV, NV), (TILE * NV) ** -0.5, 0.078125, ((2, 8), (3, 4))),
        "occ_energy": jnp.clip(jax.random.uniform(keys[4], (NOCC,), jnp.float32, -2.0, -0.5), -2.0, -0.5),
        "virt_energy": jnp.clip(jax.random.uniform(keys[5], (NV,), jnp.float32, 0.3, 3.0), 0.3, 3.0),
        "occ_irrep": plant(jax.random.randint(keys[6], (NOCC,), 0, 2), jax.random.fold_in(keys[6], 1), 0, 1).astype(jnp.int32),
        "virt_irrep": plant(jax.random.randint(keys[7], (NV // VBLK,), 0, 2), jax.random.fold_in(keys[7], 1), 0, 1).astype(jnp.int32),
        "slab_i": plant(jax.random.randint(keys[8], (NI,), 0, NOCC), jax.random.fold_in(keys[8], 1), 0, NOCC - 1).astype(jnp.int32),
        "slab_j": jax.random.randint(keys[9], (NJ,), 0, NOCC).astype(jnp.int32),
    }


def reference(amplitudes, pair_integrals, cycle_integrals, ladder_integrals, occ_energy, virt_energy, occ_irrep, virt_irrep, slab_i, slab_j):
    cycle_full = cycle_integrals.astype(jnp.float32)

    def cycle_slice(amp_row):
        return jnp.einsum("kcb,kcja->jab", amp_row.astype(jnp.float32), cycle_full).astype(jnp.bfloat16)

    cycle = lax.map(cycle_slice, amplitudes)
    tile_amps = amplitudes[:, :, :TILE, :].astype(jnp.float32)
    ladder = jnp.einsum("ijcd,acbd->ijab", tile_amps, ladder_integrals.astype(jnp.float32))
    coupled = cycle.astype(jnp.float32).at[:, :, :TILE, :].add(ladder).astype(jnp.bfloat16)
    energy_first = occ_energy[slab_i]
    energy_second = occ_energy[slab_j]
    label_first = occ_irrep[slab_i]
    label_second = occ_irrep[slab_j]
    label_virt = jnp.repeat(virt_irrep, VBLK)
    residual = pair_integrals.astype(jnp.float32) + coupled.astype(jnp.float32)
    denominator = (virt_energy[None, None, :, None] + virt_energy[None, None, None, :]
                   - energy_first[:, None, None, None] - energy_second[None, :, None, None])
    parity = (label_first[:, None, None, None] + label_second[None, :, None, None]
              + label_virt[None, None, :, None] + label_virt[None, None, None, :]) % 2
    allowed = (1 - parity).astype(jnp.float32)
    return (allowed * residual / denominator).astype(jnp.bfloat16)
```

```python
import functools

import jax
import jax.numpy as jnp
from jax import lax
from jax.experimental import pallas as pl
from jax.experimental.pallas import tpu as pltpu
from jax.sharding import PartitionSpec as P

VBLK = 16
CORE, XBIT, YBIT = 1, 2, 4
LANES = 512
VMEM = 60 * 2**20


def spread(value, axis, source):
    kept = jnp.where(lax.axis_index(axis) == source, value, 0).astype(value.dtype)
    return lax.psum(kept, axis)


def lookup(indices, values_table):
    table_size = values_table.shape[0]
    matches = indices[:, None] == jnp.arange(table_size, dtype=jnp.int32)[None, :]
    return jnp.sum(
        jnp.where(matches, values_table[None, :], jnp.zeros_like(values_table)[None, :]), axis=1
    )


def cycle_product(amp_rows, weights):
    inner_k, inner_c, outer_j, outer_a = weights.shape
    flat_weights = weights.reshape(inner_k * inner_c, outer_j * outer_a)

    def one_row(amp_row):
        flat_row = amp_row.reshape(inner_k * inner_c, amp_row.shape[2])
        product = lax.dot_general(
            flat_weights, flat_row, (((0,), (0,)), ((), ())), preferred_element_type=jnp.float32
        )
        return product.reshape(outer_j, outer_a, amp_row.shape[2]).astype(jnp.bfloat16)

    return lax.map(one_row, amp_rows)


def per_device_any(
    amplitudes,
    pair_integrals,
    cycle_integrals,
    ladder_integrals,
    occ_energy,
    virt_energy,
    occ_irrep,
    virt_irrep,
    slab_i,
    slab_j,
):
    wide_count = lax.axis_size("wide")
    wide_index = lax.axis_index("wide")
    tile_width = ladder_integrals.shape[0]
    virt_count = virt_energy.shape[0]
    row_count = virt_count // wide_count
    relaid = lax.all_to_all(amplitudes, "wide", split_axis=3, concat_axis=2, tiled=True)
    tile_amps = spread(amplitudes[:, :, :tile_width, :], "wide", 0)
    ladder = jnp.einsum(
        "ijcd,acbd->ijab",
        tile_amps,
        lax.all_gather(ladder_integrals, "narrow", axis=3, tiled=True),
        preferred_element_type=jnp.float32,
    )
    cycle_local = cycle_product(
        relaid, lax.all_gather(cycle_integrals, "narrow", axis=3, tiled=True)
    )
    coupled_local = (
        cycle_local.astype(jnp.float32).at[:, :, :tile_width, :].add(ladder).astype(jnp.bfloat16)
    )
    coupled = lax.all_to_all(coupled_local, "wide", split_axis=2, concat_axis=3, tiled=True)
    energy_first = lookup(slab_i, occ_energy)
    energy_second = lookup(slab_j, occ_energy)
    label_first = lookup(slab_i, occ_irrep)
    label_second = lookup(slab_j, occ_irrep)
    label_virt = jnp.repeat(virt_irrep, VBLK)
    energy_rows = lax.dynamic_slice_in_dim(virt_energy, wide_index * row_count, row_count)
    label_rows = lax.dynamic_slice_in_dim(label_virt, wide_index * row_count, row_count)
    residual = pair_integrals.astype(jnp.float32) + coupled.astype(jnp.float32)
    denominator = (
        energy_rows[None, None, :, None]
        + virt_energy[None, None, None, :]
        - energy_first[:, None, None, None]
        - energy_second[None, :, None, None]
    )
    parity = (
        label_first[:, None, None, None]
        + label_second[None, :, None, None]
        + label_rows[None, None, :, None]
        + label_virt[None, None, None, :]
    ) % 2
    allowed = (1 - parity).astype(jnp.float32)
    return (allowed * residual / denominator).astype(jnp.bfloat16)


def launch_kernel(extended, passed, *refs):
    outs = refs[len(refs) - len(extended) - passed :]
    for out, extra in zip(outs, extended):
        rows = refs[0].shape[2]
        out[0, 0, pl.ds(0, rows), :] = refs[0][0, 0]
        if extra:
            out[0, 0, pl.ds(rows, out.shape[2] - rows), :] = refs[1][0, 0]
        refs = refs[1 + extra :]


def launch(cuts, handed_on, waited_for):
    anywhere = pl.BlockSpec(memory_space=pl.ANY)
    operands, in_specs, out_specs, out_shape = [], [], [], []
    second = 1
    for array, index, extra in cuts:
        _, second, rows, cols = array.shape
        operands.append(array)
        in_specs.append(pl.BlockSpec((1, 1, rows, cols), lambda j, index=index: (index, j, 0, 0)))
        if extra is not None:
            operands.append(extra)
            in_specs.append(pl.BlockSpec((1, 1, *extra.shape[2:]), lambda j: (0, j, 0, 0)))
            rows += extra.shape[2]
        out_specs.append(pl.BlockSpec((1, 1, rows, cols), lambda j: (0, j, 0, 0)))
        out_shape.append(jax.ShapeDtypeStruct((1, second, rows, cols), array.dtype))
    aliases = {len(operands) + n: len(cuts) + n for n in range(len(handed_on))}
    in_specs += [anywhere for _ in [*handed_on, *waited_for]]
    out_specs += [anywhere for _ in handed_on]
    out_shape += [jax.ShapeDtypeStruct(value.shape, value.dtype) for value in handed_on]
    outs = pl.pallas_call(
        functools.partial(launch_kernel, tuple(extra is not None for *_, extra in cuts), len(handed_on)),
        grid=(second,),
        out_shape=tuple(out_shape),
        in_specs=in_specs,
        out_specs=tuple(out_specs),
        input_output_aliases=aliases,
        compiler_params=pltpu.CompilerParams(vmem_limit_bytes=VMEM),
        cost_estimate=pl.CostEstimate(flops=0, bytes_accessed=1, transcendentals=0),
        name="launch",
    )(*operands, *handed_on, *waited_for)
    return list(outs[: len(cuts)]), list(outs[len(cuts) :])


def blocks_kernel(place, weights, after, out_ref, turned):
    inner_k, row_count, outer_j, _ = weights.shape
    depth = inner_k * row_count
    flat = weights[...].reshape(depth * outer_j, weights.shape[3])
    row = lax.broadcasted_iota(jnp.int32, (depth * outer_j, depth), 0)
    col = lax.broadcasted_iota(jnp.int32, (depth * outer_j, depth), 1)
    mine = pl.ds(pl.multiple_of(place[1] * row_count, row_count), row_count)
    for j in range(outer_j):
        picked = (row == outer_j * col + j).astype(weights.dtype)
        turned[...] = lax.dot_general(flat, picked, (((0,), (0,)), ((), ())), preferred_element_type=jnp.float32)
        out_ref[0, pl.ds(j * row_count, row_count), :] = turned[mine, :].astype(out_ref.dtype)


def weight_blocks(first, core, count, cycle_integrals, row_count, after):
    inner_k, _, outer_j, width = cycle_integrals.shape
    shape = (outer_j * row_count, inner_k * row_count)
    return pl.pallas_call(
        blocks_kernel,
        out_shape=jax.ShapeDtypeStruct((count, *shape), cycle_integrals.dtype),
        grid_spec=pltpu.PrefetchScalarGridSpec(
            num_scalar_prefetch=1,
            grid=(count,),
            in_specs=[
                pl.BlockSpec((inner_k, row_count, outer_j, width), lambda n, s: (0, s[0] + n, 0, 0)),
                pl.BlockSpec(memory_space=pl.ANY),
            ],
            out_specs=pl.BlockSpec((1, *shape), lambda n, s: (n, 0, 0)),
            scratch_shapes=[pltpu.VMEM((width, shape[1]), jnp.float32)],
        ),
        compiler_params=pltpu.CompilerParams(vmem_limit_bytes=VMEM),
        cost_estimate=pl.CostEstimate(
            flops=0, bytes_accessed=6 * count * shape[0] * shape[1], transcendentals=0
        ),
        name="weight_blocks",
    )(jnp.stack([first, core]).astype(jnp.int32), cycle_integrals, after)


def partial_kernel(sources, scalars, *refs):
    weights, (own, beside, near, far, send_ref, keep_ref) = refs[:-6], refs[-6:]
    half = len(weights) // 2
    depth = own.shape[1] * own.shape[2]
    pieces = [piece[0].reshape(depth, piece.shape[3]) for piece in (own, beside, near, far)]
    rows = jnp.concatenate(pieces, axis=0)
    for out, blocks in ((send_ref, weights[:half]), (keep_ref, weights[half:])):
        matrix = jnp.concatenate([blocks[source][0, scalars[2 + n]] for n, source in enumerate(sources)], axis=1)
        product = jnp.dot(matrix, rows, preferred_element_type=jnp.float32)
        out[0] = product.astype(out.dtype).reshape(out.shape[1:])


def partial_sums(scalars, sources, weights, amplitudes, index, beside, near, far):
    _, second, rows, cols = amplitudes.shape
    lanes = min(LANES, cols)
    out_rows, depth = weights[0].shape[2:]
    piece = pl.BlockSpec((1, second, rows, lanes), lambda n, s: (0, 0, 0, n))
    mine = pl.BlockSpec((1, second, rows, lanes), lambda n, s: (index, 0, 0, n))
    for_neighbour = [pl.BlockSpec((1, *w.shape[1:]), lambda n, s: (s[0], 0, 0, 0)) for w in weights]
    for_self = [pl.BlockSpec((1, *w.shape[1:]), lambda n, s: (s[1], 0, 0, 0)) for w in weights]
    return pl.pallas_call(
        functools.partial(partial_kernel, sources),
        out_shape=(
            jax.ShapeDtypeStruct((1, second, rows, cols), jnp.bfloat16),
            jax.ShapeDtypeStruct((1, second, rows, cols), jnp.float32),
        ),
        grid_spec=pltpu.PrefetchScalarGridSpec(
            num_scalar_prefetch=1,
            grid=(cols // lanes,),
            in_specs=[*for_neighbour, *for_self, mine, mine, piece, piece],
            out_specs=(piece, piece),
        ),
        compiler_params=pltpu.CompilerParams(vmem_limit_bytes=VMEM),
        cost_estimate=pl.CostEstimate(
            flops=16 * out_rows * depth * cols,
            bytes_accessed=14 * second * rows * cols + 16 * out_rows * depth,
            transcendentals=0,
        ),
        name="partial_sums",
    )(scalars, *weights, *weights, amplitudes, beside, near, far)


def finish_kernel(
    index, e_first, e_second, l_first, l_second, keep, arrived, pair, ladder, e_rows, l_rows, e_cols, l_cols, *rest
):
    out_ref, token_ref, coupled = rest[-3:]
    second = pl.program_id(0)
    top = ladder.shape[1]
    cycle = (keep[0, 0] + arrived[0, 0].astype(jnp.float32)).astype(jnp.bfloat16)
    coupled[...] = cycle.astype(jnp.float32)
    with_ladder = coupled[pl.ds(0, top), :] + ladder[0]
    coupled[pl.ds(0, top), :] = with_ladder.astype(jnp.bfloat16).astype(jnp.float32)
    residual = pair[0, 0].astype(jnp.float32) + coupled[...]
    denominator = (e_rows[...] - e_first[index] - e_second[second]) + e_cols[...]
    odd_rows = (l_rows[...] + l_first[index] + l_second[second]) & 1
    value = jnp.where(odd_rows == l_cols[...] & 1, residual / denominator, 0.0)
    out_ref[0, 0] = value.astype(jnp.bfloat16)
    token_ref[...] = jnp.zeros_like(token_ref)


def finish(index, occupied, keep, arrived, pair_integrals, ladder, virtual, so_far):
    count, second, rows, cols = pair_integrals.shape
    lanes = cols
    top = ladder.shape[1]
    one = pl.BlockSpec((1, 1, rows, lanes), lambda j, n, *s: (0, j, 0, n))
    at_index = pl.BlockSpec((1, 1, rows, lanes), lambda j, n, *s: (index, j, 0, n))
    by_row = pl.BlockSpec((rows, 1), lambda j, n, *s: (0, 0))
    by_col = pl.BlockSpec((1, lanes), lambda j, n, *s: (0, n))
    operands = [*occupied, keep, arrived, pair_integrals, ladder, *virtual]
    in_specs = [
        one,
        one,
        at_index,
        pl.BlockSpec((1, top, lanes), lambda j, n, *s: (index * second + j, 0, n)),
        by_row,
        by_row,
        by_col,
        by_col,
    ]
    aliases = {}
    if so_far is not None:
        aliases = {len(operands): 0}
        operands.append(so_far)
        in_specs.append(pl.BlockSpec(memory_space=pl.ANY))
    return pl.pallas_call(
        functools.partial(finish_kernel, index),
        out_shape=(
            jax.ShapeDtypeStruct(pair_integrals.shape, jnp.bfloat16),
            jax.ShapeDtypeStruct((8, 128), jnp.float32),
        ),
        grid_spec=pltpu.PrefetchScalarGridSpec(
            num_scalar_prefetch=4,
            grid=(second, cols // lanes),
            in_specs=in_specs,
            out_specs=(at_index, pl.BlockSpec((8, 128), lambda j, n, *s: (0, 0))),
            scratch_shapes=[pltpu.VMEM((rows, lanes), jnp.float32)],
        ),
        input_output_aliases=aliases,
        compiler_params=pltpu.CompilerParams(vmem_limit_bytes=VMEM),
        cost_estimate=pl.CostEstimate(
            flops=12 * second * rows * cols, bytes_accessed=10 * second * rows * cols, transcendentals=0
        ),
        name="finish",
    )(*operands)


def per_device_plane(
    amplitudes,
    pair_integrals,
    cycle_integrals,
    ladder_integrals,
    occ_energy,
    virt_energy,
    occ_irrep,
    virt_irrep,
    slab_i,
    slab_j,
):
    wide_count, narrow_count = lax.axis_size("wide"), lax.axis_size("narrow")
    wide_index = lax.axis_index("wide")
    core, x, y = wide_index % 2, wide_index // 2 % 2, wide_index // 4
    count, second, row_count, virt_count = amplitudes.shape
    tile_width, _, _, ladder_depth = ladder_integrals.shape
    tile_rows = count * second * tile_width

    def across(value, bit):
        return lax.ppermute(value, "wide", [(w, w ^ bit) for w in range(wide_count)])

    by_y = count * 5 // 12
    first_x, first_y = list(range(count - by_y)), list(range(count - by_y, count))
    x_queue = [("gather", n) for n in first_x] + [("sum", n) for n in first_y]
    y_queue = [("gather", n) for n in first_y] + [("sum", n) for n in first_x]

    tile = amplitudes[:, :, :tile_width, :].reshape(tile_rows, virt_count)
    to_x, to_y, to_both = (lax.ppermute(tile, "wide", [(0, w)]) for w in (XBIT, YBIT, XBIT + YBIT))

    near_blocks = weight_blocks(4 * y, core, 4, cycle_integrals, row_count, tile)
    same_row = lax.all_gather(near_blocks, "narrow", axis=0)
    in_row = (x * 2 + core, x * 2 + 1 - core)
    numbers_x = jnp.stack(
        [2 * (1 - y) + x, 2 * y + x, *in_row, (1 - x) * 2 + core, (1 - x) * 2 + 1 - core]
    ).astype(jnp.int32)
    numbers_y = jnp.stack([2 * y + 1 - x, 2 * y + x, *in_row, core, 1 - core]).astype(jnp.int32)

    label_virt = jnp.repeat(virt_irrep, VBLK)
    energy_rows = lax.dynamic_slice_in_dim(virt_energy, wide_index * row_count, row_count)
    label_rows = lax.dynamic_slice_in_dim(label_virt, wide_index * row_count, row_count)
    occupied = (
        lookup(slab_i, occ_energy),
        lookup(slab_j, occ_energy),
        lookup(slab_i, occ_irrep),
        lookup(slab_j, occ_irrep),
    )
    virtual = (energy_rows[:, None], label_rows[:, None], virt_energy[None, :], label_virt[None, :])

    near, far, sends, kept, tokens = {}, {}, {}, {}, {}

    def sums(index):
        if index not in sends:
            if index in first_x:
                plan = (numbers_x, (0, 0, 0, 0), (same_row,))
            else:
                plan = (numbers_y, (0, 0, 1, 1), (same_row, other_row))
            sends[index], kept[index] = partial_sums(
                *plan, amplitudes, index, beside, near[index], far[index]
            )
        return sends[index]

    def ladder_amplitudes():
        corner = jnp.where(x == 0, jnp.where(y == 0, tile, to_y), jnp.where(y == 0, to_x, to_both))
        other = lax.ppermute(corner, "wide", [(w, w + CORE) for w in range(0, wide_count, 2)])
        every = jnp.where(core == 0, corner, other)
        every = every.reshape(tile_rows, narrow_count, ladder_depth).transpose(1, 0, 2)
        return lax.all_to_all(every, "narrow", split_axis=0, concat_axis=0, tiled=True)

    def ladder_chip(every):
        every = every.reshape(-1, tile_width, ladder_depth)
        part = jnp.einsum("xcd,acbd->xab", every, ladder_integrals, preferred_element_type=jnp.float32)
        part = part.reshape(narrow_count, tile_rows, row_count)
        part = lax.all_to_all(part, "narrow", split_axis=0, concat_axis=0, tiled=True).sum(axis=0)
        other = lax.ppermute(part, "wide", [(w + CORE, w) for w in range(0, wide_count, 2)])
        return jnp.concatenate([part, other], axis=1).astype(jnp.bfloat16)

    def packed(value):
        pieces = virt_count // value.shape[1]
        flat = jnp.concatenate(jnp.split(value, pieces), axis=1)
        rows = -(-flat.shape[0] // (16 * second)) * 16
        return jnp.pad(flat, ((0, rows * second - flat.shape[0]), (0, 0))).reshape(1, second, rows, virt_count)

    def unpacked(value, width):
        flat = value[:, :, row_count:, :].reshape(-1, virt_count)
        pieces = virt_count // width
        return jnp.concatenate(jnp.split(flat[: tile_rows // pieces], pieces, axis=1))

    x_slot, y_slot = 5, 7
    out, ladder = None, None
    moved, forwarded, arrived_at, waiting = [], [], [], []
    for slot in range(count):
        due = [(XBIT, *x_queue[slot]), (YBIT, *y_queue[slot])]
        waits, extras, handed_on = [], {}, []
        if slot == 0:
            waits += [near_blocks, to_x, to_y, to_both]
        if slot == 1:
            waits += [*operands, far_blocks, beside, *occupied, *virtual]
        if slot >= 2:
            waits += moved[slot - 2]
        if slot >= 3:
            waits += forwarded[slot - 3]
        if slot == 3:
            handed_on = [tile_amps]
        if slot == x_slot:
            extras = {XBIT: packed(chip_part)}
        if slot == y_slot:
            row_part = jnp.concatenate([chip_part, unpacked(moved[x_slot][0], chip_part.shape[1])], axis=1)
            extras = {YBIT: packed(row_part)}
        if slot >= by_y and slot + 1 < count:
            sums(y_queue[slot + 1][1])
            waits.append(kept[y_queue[slot + 1][1]])
        if slot >= 9:
            waits += [tokens[n] for at in arrived_at[: slot - 3] for n in at]
        cuts = [
            (amplitudes, index, extras.get(bit)) if kind == "gather" else (sums(index), 0, extras.get(bit))
            for bit, kind, index in due
        ]
        plain = [n for n, (bit, kind, _) in enumerate(due) if kind == "sum" and bit not in extras]
        sent, passed = launch(
            [cut for n, cut in enumerate(cuts) if n not in plain], [cuts[n][0] for n in plain] + handed_on, waits
        )
        operands = [passed.pop(0) if n in plain else sent.pop(0) for n in range(len(due))]
        if slot == 0:
            beside = across(amplitudes, CORE)
            far_blocks = weight_blocks(4 * (1 - y) + 2 * x, core, 2, cycle_integrals, row_count, operands[0])
            other_row = lax.all_gather(far_blocks, "narrow", axis=0)
            tile_amps = ladder_amplitudes()
        if slot == 3:
            chip_part = ladder_chip(passed[0])
        moved.append([])
        forwarded.append([])
        arrived_at.append([])
        for operand, (bit, kind, index) in zip(operands, due):
            value = across(operand, bit)
            moved[-1].append(value)
            if kind == "gather":
                near[index], far[index] = value, across(value, CORE)
                forwarded[-1].append(far[index])
            else:
                arrived_at[-1].append(index)
                waiting.append((index, value))
        if slot == y_slot:
            parts = [row_part, unpacked(moved[y_slot][1], row_part.shape[1])]
            ladder = jnp.where(wide_index == 0, jnp.concatenate(parts, axis=1).astype(jnp.float32), 0.0)
            ladder = ladder.reshape(count * second, tile_width, virt_count)
        while waiting and slot >= y_slot:
            index, value = waiting.pop(0)
            out, tokens[index] = finish(
                index, occupied, kept[index], value, pair_integrals, ladder, virtual, out
            )
    return out


def solution(mesh):
    wide, narrow = mesh.shape["wide"], mesh.shape["narrow"]
    per_device = per_device_plane if (wide, narrow) == (8, 4) else per_device_any
    return jax.shard_map(
        per_device,
        mesh=mesh,
        in_specs=(
            P("narrow", None, "wide", None),
            P("narrow", None, "wide", None),
            P(None, None, None, "narrow"),
            P(None, None, "wide", "narrow"),
            P(),
            P(),
            P(),
            P(),
            P("narrow"),
            P(),
        ),
        out_specs=P("narrow", None, "wide", None),
        check_vma=False,
    )
```

```python
import functools

import jax
import jax.numpy as jnp
from jax import lax
from jax.experimental import pallas as pl
from jax.experimental.pallas import tpu as pltpu
from jax.sharding import PartitionSpec as P

VBLK = 16
CORE, XBIT, YBIT = 1, 2, 4
LANES = 512
VMEM = 60 * 2**20
COST = pl.CostEstimate(flops=0, bytes_accessed=1, transcendentals=0)


def spread(value, axis, source):
    kept = jnp.where(lax.axis_index(axis) == source, value, 0).astype(value.dtype)
    return lax.psum(kept, axis)


def lookup(indices, values_table):
    table_size = values_table.shape[0]
    matches = indices[:, None] == jnp.arange(table_size, dtype=jnp.int32)[None, :]
    return jnp.sum(
        jnp.where(matches, values_table[None, :], jnp.zeros_like(values_table)[None, :]), axis=1
    )


def cycle_product(amp_rows, weights):
    inner_k, inner_c, outer_j, outer_a = weights.shape
    flat_weights = weights.reshape(inner_k * inner_c, outer_j * outer_a)

    def one_row(amp_row):
        flat_row = amp_row.reshape(inner_k * inner_c, amp_row.shape[2])
        product = lax.dot_general(
            flat_weights, flat_row, (((0,), (0,)), ((), ())), preferred_element_type=jnp.float32
        )
        return product.reshape(outer_j, outer_a, amp_row.shape[2]).astype(jnp.bfloat16)

    return lax.map(one_row, amp_rows)


def per_device_any(
    amplitudes,
    pair_integrals,
    cycle_integrals,
    ladder_integrals,
    occ_energy,
    virt_energy,
    occ_irrep,
    virt_irrep,
    slab_i,
    slab_j,
):
    wide_count = lax.axis_size("wide")
    wide_index = lax.axis_index("wide")
    tile_width = ladder_integrals.shape[0]
    virt_count = virt_energy.shape[0]
    row_count = virt_count // wide_count
    relaid = lax.all_to_all(amplitudes, "wide", split_axis=3, concat_axis=2, tiled=True)
    tile_amps = spread(amplitudes[:, :, :tile_width, :], "wide", 0)
    ladder = jnp.einsum(
        "ijcd,acbd->ijab",
        tile_amps,
        lax.all_gather(ladder_integrals, "narrow", axis=3, tiled=True),
        preferred_element_type=jnp.float32,
    )
    cycle_local = cycle_product(
        relaid, lax.all_gather(cycle_integrals, "narrow", axis=3, tiled=True)
    )
    coupled_local = (
        cycle_local.astype(jnp.float32).at[:, :, :tile_width, :].add(ladder).astype(jnp.bfloat16)
    )
    coupled = lax.all_to_all(coupled_local, "wide", split_axis=2, concat_axis=3, tiled=True)
    energy_first = lookup(slab_i, occ_energy)
    energy_second = lookup(slab_j, occ_energy)
    label_first = lookup(slab_i, occ_irrep)
    label_second = lookup(slab_j, occ_irrep)
    label_virt = jnp.repeat(virt_irrep, VBLK)
    energy_rows = lax.dynamic_slice_in_dim(virt_energy, wide_index * row_count, row_count)
    label_rows = lax.dynamic_slice_in_dim(label_virt, wide_index * row_count, row_count)
    residual = pair_integrals.astype(jnp.float32) + coupled.astype(jnp.float32)
    denominator = (
        energy_rows[None, None, :, None]
        + virt_energy[None, None, None, :]
        - energy_first[:, None, None, None]
        - energy_second[None, :, None, None]
    )
    parity = (
        label_first[:, None, None, None]
        + label_second[None, :, None, None]
        + label_rows[None, None, :, None]
        + label_virt[None, None, None, :]
    ) % 2
    allowed = (1 - parity).astype(jnp.float32)
    return (allowed * residual / denominator).astype(jnp.bfloat16)


def cut_kernel(copies, passed, *refs):
    outs = refs[len(refs) - copies - passed :]
    for source, out in zip(refs[:copies], outs):
        out[...] = source[...]


def cut(amplitudes, pairs, handed_on, waited_for):
    anywhere = pl.BlockSpec(memory_space=pl.ANY)
    _, second, rows, cols = amplitudes.shape
    block = (2, 1, rows, cols)
    copies = len(pairs)
    outs = pl.pallas_call(
        functools.partial(cut_kernel, copies, len(handed_on)),
        grid=(second if copies else 1,),
        out_shape=(
            *(jax.ShapeDtypeStruct((2, second, rows, cols), amplitudes.dtype) for _ in pairs),
            *(jax.ShapeDtypeStruct(value.shape, value.dtype) for value in handed_on),
        ),
        in_specs=[
            *(pl.BlockSpec(block, lambda j, n=n: (n, j, 0, 0)) for n in pairs),
            *(anywhere for _ in [*handed_on, *waited_for]),
        ],
        out_specs=(
            *(pl.BlockSpec(block, lambda j: (0, j, 0, 0)) for _ in pairs),
            *(anywhere for _ in handed_on),
        ),
        input_output_aliases={copies + n: copies + n for n in range(len(handed_on))},
        compiler_params=pltpu.CompilerParams(vmem_limit_bytes=VMEM),
        cost_estimate=COST,
        name="cut",
    )(*[amplitudes] * copies, *handed_on, *waited_for)
    return outs[:copies], outs[copies:]


def blocks_kernel(place, weights, after, out_ref, handed, turned, picked):
    inner_k, row_count, outer_j, _ = weights.shape
    depth = inner_k * row_count
    flat = weights[...].reshape(depth * outer_j, weights.shape[3])
    mine = pl.ds(pl.multiple_of(place[1] * row_count, row_count), row_count)

    @pl.when(pl.program_id(0) == 0)
    def _():
        row = lax.broadcasted_iota(jnp.int32, picked.shape[1:], 0)
        col = lax.broadcasted_iota(jnp.int32, picked.shape[1:], 1)
        for j in range(outer_j):
            picked[j] = (row == outer_j * col + j).astype(picked.dtype)

    for j in range(outer_j):
        turned[...] = lax.dot_general(flat, picked[j], (((0,), (0,)), ((), ())), preferred_element_type=jnp.float32)
        out_ref[0, pl.ds(j * row_count, row_count), :] = turned[mine, :].astype(out_ref.dtype)


def weight_blocks(first, core, count, cycle_integrals, row_count, after):
    inner_k, _, outer_j, width = cycle_integrals.shape
    shape = (outer_j * row_count, inner_k * row_count)
    return pl.pallas_call(
        blocks_kernel,
        out_shape=(
            jax.ShapeDtypeStruct((count, *shape), cycle_integrals.dtype),
            jax.ShapeDtypeStruct(after.shape, after.dtype),
        ),
        grid_spec=pltpu.PrefetchScalarGridSpec(
            num_scalar_prefetch=1,
            grid=(count,),
            in_specs=[
                pl.BlockSpec((inner_k, row_count, outer_j, width), lambda n, s: (0, s[0] + n, 0, 0)),
                pl.BlockSpec(memory_space=pl.ANY),
            ],
            out_specs=(pl.BlockSpec((1, *shape), lambda n, s: (n, 0, 0)), pl.BlockSpec(memory_space=pl.ANY)),
            scratch_shapes=[
                pltpu.VMEM((width, shape[1]), jnp.float32),
                pltpu.VMEM((outer_j, shape[1] * outer_j, shape[1]), cycle_integrals.dtype),
            ],
        ),
        input_output_aliases={2: 1},
        compiler_params=pltpu.CompilerParams(vmem_limit_bytes=VMEM),
        cost_estimate=COST,
        name="weight_blocks",
    )(jnp.stack([first, core]).astype(jnp.int32), cycle_integrals, after)


def partial_kernel(sources, outs, scalars, *refs):
    blocks = len(set(sources))
    for_neighbour, for_self, refs = refs[:blocks], refs[blocks : 2 * blocks], refs[2 * blocks :]
    own, beside, near, far = refs[:4]
    *send, keep = refs[len(refs) - outs :]
    depth = own.shape[1] * own.shape[2]
    for unit in range(2):
        rows = [piece[unit].reshape(depth, piece.shape[3]) for piece in (own, beside, near, far)]
        rows = jnp.concatenate(rows, axis=0)
        to_send = send[0].at[unit] if len(send) == 1 else send[unit].at[0]
        for out, weights in ((to_send, for_neighbour), (keep.at[unit], for_self)):
            matrix = [weights[source][0, scalars[2 + n]] for n, source in enumerate(sources)]
            product = jnp.dot(jnp.concatenate(matrix, axis=1), rows, preferred_element_type=jnp.float32)
            out[...] = product.astype(out.dtype).reshape(out.shape)


def partial_sums(scalars, sources, weights, amplitudes, beside, near, far, pair, apart, waited_for):
    _, second, rows, cols = amplitudes.shape
    lanes = min(LANES, cols)
    out_rows, depth = weights[0].shape[2:]
    mine = pl.BlockSpec((2, second, rows, lanes), lambda n, s: (pair, 0, 0, n))
    both = pl.BlockSpec((2, second, rows, lanes), lambda n, s: (0, 0, 0, n))
    one = pl.BlockSpec((1, second, rows, lanes), lambda n, s: (0, 0, 0, n))
    for_neighbour = [pl.BlockSpec((1, *w.shape[1:]), lambda n, s: (s[0], 0, 0, 0)) for w in weights]
    for_self = [pl.BlockSpec((1, *w.shape[1:]), lambda n, s: (s[1], 0, 0, 0)) for w in weights]
    two = (2, second, rows, cols)
    send_shapes = [(1, *two[1:])] * 2 if apart else [two]
    outs = pl.pallas_call(
        functools.partial(partial_kernel, sources, len(send_shapes) + 1),
        out_shape=(
            *(jax.ShapeDtypeStruct(shape, jnp.bfloat16) for shape in send_shapes),
            jax.ShapeDtypeStruct(two, jnp.float32),
        ),
        grid_spec=pltpu.PrefetchScalarGridSpec(
            num_scalar_prefetch=1,
            grid=(cols // lanes,),
            in_specs=[
                *(*for_neighbour, *for_self, mine, mine, both, both),
                *(pl.BlockSpec(memory_space=pl.ANY) for _ in waited_for),
            ],
            out_specs=(*([one, one] if apart else [both]), both),
        ),
        compiler_params=pltpu.CompilerParams(vmem_limit_bytes=VMEM),
        cost_estimate=COST,
        name="partial_sums",
    )(scalars, *weights, *weights, amplitudes, beside, near, far, *waited_for)
    return outs[:-1], outs[-1]


def finish_kernel(indices, second_count, slab_i, slab_j, occ_energy, occ_irrep, *refs):
    units = len(indices)
    sums, refs = refs[: 2 * units], refs[2 * units :]
    pair, ladder, e_rows, l_rows, e_cols, l_cols = refs[:6]
    out_ref, token_ref, coupled = refs[-3:]
    second = pl.program_id(1)
    top = ladder.shape[0] // second_count
    for unit, index in enumerate(indices):
        keep, arrived = sums[2 * unit : 2 * unit + 2]

        @pl.when(pl.program_id(0) == unit)
        def _(index=index, keep=keep, arrived=arrived):
            cycle = (keep[0, 0] + arrived[0, 0].astype(jnp.float32)).astype(jnp.bfloat16)
            coupled[...] = cycle.astype(jnp.float32)
            mine = ladder[pl.ds(0, top), :]
            for j in range(1, ladder.shape[0] // top):
                mine = jnp.where(second == j, ladder[pl.ds(j * top, top), :], mine)
            with_ladder = coupled[pl.ds(0, top), :] + mine
            coupled[pl.ds(0, top), :] = with_ladder.astype(jnp.bfloat16).astype(jnp.float32)
            residual = pair[0, 0].astype(jnp.float32) + coupled[...]
            denominator = (e_rows[...] - occ_energy[slab_i[index]] - occ_energy[slab_j[second]]) + e_cols[...]
            odd_rows = (l_rows[...] + occ_irrep[slab_i[index]] + occ_irrep[slab_j[second]]) & 1
            value = jnp.where(odd_rows == l_cols[...] & 1, residual / denominator, 0.0)
            out_ref[0, 0] = value.astype(jnp.bfloat16)

    token_ref[...] = jnp.zeros_like(token_ref)


def finish(occupied, units, pair_integrals, ladder, virtual, so_far, after):
    _, second, rows, cols = pair_integrals.shape
    top = ladder.shape[0] // pair_integrals.shape[0]
    indices = tuple(index for index, *_ in units)
    step = indices[-1] - indices[0]
    block = (1, 1, rows, cols)
    at_index = pl.BlockSpec(block, lambda u, j, *s: (indices[0] + u * step, j, 0, 0))
    by_row = pl.BlockSpec((rows, 1), lambda u, j, *s: (0, 0))
    by_col = pl.BlockSpec((1, cols), lambda u, j, *s: (0, 0))
    operands, in_specs = [*occupied], []
    for unit, (_, *arrays) in enumerate(units):
        for array, place in arrays:
            own = lambda u, j, *s, unit=unit, place=place: (
                place,
                jnp.where(u == unit, j, jnp.where(u < unit, 0, second - 1)),
                0,
                0,
            )
            operands.append(array)
            in_specs.append(pl.BlockSpec(block, own))
    operands += [pair_integrals, ladder, *virtual]
    in_specs += [
        at_index,
        pl.BlockSpec((top, cols), lambda u, j, *s: (indices[0] + u * step, 0)),
        by_row,
        by_row,
        by_col,
        by_col,
    ]
    operands.append(after)
    in_specs.append(pl.BlockSpec(memory_space=pl.ANY))
    aliases = {}
    if so_far is not None:
        aliases = {len(operands): 0}
        operands.append(so_far)
        in_specs.append(pl.BlockSpec(memory_space=pl.ANY))
    return pl.pallas_call(
        functools.partial(finish_kernel, indices, second),
        out_shape=(
            jax.ShapeDtypeStruct(pair_integrals.shape, jnp.bfloat16),
            jax.ShapeDtypeStruct((8, 128), jnp.float32),
        ),
        grid_spec=pltpu.PrefetchScalarGridSpec(
            num_scalar_prefetch=4,
            grid=(len(units), second),
            in_specs=in_specs,
            out_specs=(at_index, pl.BlockSpec((8, 128), lambda u, j, *s: (0, 0))),
            scratch_shapes=[pltpu.VMEM((rows, cols), jnp.float32)],
        ),
        input_output_aliases=aliases,
        compiler_params=pltpu.CompilerParams(vmem_limit_bytes=VMEM),
        cost_estimate=COST,
        name="finish",
    )(*operands)


def per_device_plane(
    amplitudes,
    pair_integrals,
    cycle_integrals,
    ladder_integrals,
    occ_energy,
    virt_energy,
    occ_irrep,
    virt_irrep,
    slab_i,
    slab_j,
):
    wide_count, narrow_count = lax.axis_size("wide"), lax.axis_size("narrow")
    wide_index = lax.axis_index("wide")
    core, x, y = wide_index % 2, wide_index // 2 % 2, wide_index // 4
    count, second, row_count, virt_count = amplitudes.shape
    tile_width, _, _, ladder_depth = ladder_integrals.shape
    tile_rows = count * second * tile_width

    def across(value, bit):
        return lax.ppermute(value, "wide", [(w, w ^ bit) for w in range(wide_count)])

    tile = amplitudes[:, :, :tile_width, :].reshape(tile_rows, virt_count)
    near_blocks, tile = weight_blocks(4 * y, core, 4, cycle_integrals, row_count, tile)
    same_row = lax.all_gather(near_blocks, "narrow", axis=0)
    to_x, to_y, to_both = (lax.ppermute(tile, "wide", [(0, w)]) for w in (XBIT, YBIT, XBIT + YBIT))
    in_row = (x * 2 + core, x * 2 + 1 - core)
    numbers_x = jnp.stack(
        [2 * (1 - y) + x, 2 * y + x, *in_row, (1 - x) * 2 + core, (1 - x) * 2 + 1 - core]
    ).astype(jnp.int32)
    numbers_y = jnp.stack([2 * y + 1 - x, 2 * y + x, *in_row, core, 1 - core]).astype(jnp.int32)

    label_virt = jnp.repeat(virt_irrep, VBLK)
    energy_rows = lax.dynamic_slice_in_dim(virt_energy, wide_index * row_count, row_count)
    label_rows = lax.dynamic_slice_in_dim(label_virt, wide_index * row_count, row_count)
    occupied = (slab_i, slab_j, occ_energy, occ_irrep)
    virtual = (energy_rows[:, None], label_rows[:, None], virt_energy[None, :], label_virt[None, :])

    def ladder_amplitudes(to_x, to_y, to_both):
        corner = jnp.where(x == 0, jnp.where(y == 0, tile, to_y), jnp.where(y == 0, to_x, to_both))
        other = lax.ppermute(corner, "wide", [(w, w + CORE) for w in range(0, wide_count, 2)])
        every = jnp.where(core == 0, corner, other)
        every = every.reshape(tile_rows, narrow_count, ladder_depth).transpose(1, 0, 2)
        return lax.all_to_all(every, "narrow", split_axis=0, concat_axis=0, tiled=True)

    def ladder_product(every):
        every = every.reshape(-1, tile_width, ladder_depth)
        part = jnp.einsum("xcd,acbd->xab", every, ladder_integrals, preferred_element_type=jnp.float32)
        return part.reshape(narrow_count, tile_rows, row_count)

    def ladder_chip(part):
        part = lax.all_to_all(part, "narrow", split_axis=0, concat_axis=0, tiled=True).sum(axis=0)
        other = lax.ppermute(part, "wide", [(w + CORE, w) for w in range(0, wide_count, 2)])
        return jnp.concatenate([part, other], axis=1).astype(jnp.bfloat16)

    along_x, along_y = (0, 1, 2, 3), (4, 5)
    kept, arrived = {}, {}

    def sums(pair, pieces, waited_for):
        plan = (numbers_x, (0, 0, 0, 0), (same_row,))
        if pair in along_y:
            plan = (numbers_y, (0, 0, 1, 1), (same_row, other_row))
        last = pair in (along_x[-1], along_y[-1])
        send, kept[pair] = partial_sums(*plan, amplitudes, beside, *pieces, pair, last, waited_for)
        there = [across(value, YBIT if pair in along_x else XBIT) for value in send]
        arrived[pair] = [(there[n], 0) if last else (there[0], n) for n in range(2)]
        return send[0]

    def ends(units, so_far, waited_for):
        units = [(2 * pair + n, (kept[pair], n), arrived[pair][n]) for pair, n in units]
        return finish(occupied, units, pair_integrals, ladder, virtual, so_far, waited_for)

    first, _ = cut(amplitudes, (0, 4), [], [near_blocks, to_x, to_y, to_both])
    beside = across(amplitudes, CORE)
    near_0, near_4 = across(first[0], XBIT), across(first[1], YBIT)
    then, to_all = cut(amplitudes, (1, 5), [to_x, to_y, to_both], [*first, beside])
    near_1, near_5 = across(then[0], XBIT), across(then[1], YBIT)
    tile_amps = ladder_amplitudes(*to_all)
    _, (near_0, near_4, tile_amps) = cut(amplitudes, (), [near_0, near_4, tile_amps], [*then])
    far_0, far_4 = across(near_0, CORE), across(near_4, CORE)
    far_blocks, ladder_part = weight_blocks(
        4 * (1 - y) + 2 * x, core, 2, cycle_integrals, row_count, ladder_product(tile_amps)
    )
    other_row = lax.all_gather(far_blocks, "narrow", axis=0)
    chip_part = ladder_chip(ladder_part)
    third, _ = cut(amplitudes, (2,), [], [*then, far_0, far_4])
    near_2 = across(third[0], XBIT)
    after = sums(0, (near_0, far_0), [third[0], chip_part])
    _, (near_1, near_5, chip_part) = cut(amplitudes, (), [near_1, near_5, chip_part], [after, *virtual])
    far_1, far_5 = across(near_1, CORE), across(near_5, CORE)
    from_x = lax.ppermute(chip_part, "wide", [(w + XBIT, w) for w in (0, YBIT)])
    fourth, _ = cut(amplitudes, (3,), [], [near_1, far_1, far_5])
    near_3 = across(fourth[0], XBIT)
    after = sums(1, (near_1, far_1), [fourth[0]])
    _, (near_2, from_x) = cut(amplitudes, (), [near_2, from_x], [after, arrived[0][0][0]])
    far_2 = across(near_2, CORE)
    row_part = jnp.concatenate([chip_part, from_x], axis=1)
    from_y = lax.ppermute(row_part, "wide", [(YBIT, 0)])
    after = sums(4, (near_4, far_4), [near_2])
    after = sums(2, (near_2, far_2), [after])
    after = sums(5, (near_5, far_5), [after])
    _, (near_3, from_y) = cut(amplitudes, (), [near_3, from_y], [after, arrived[1][0][0]])
    far_3 = across(near_3, CORE)
    ladder = jnp.concatenate([row_part, from_y], axis=1).astype(jnp.float32)
    ladder = jnp.where(wide_index == 0, ladder, 0.0)
    after = sums(3, (near_3, far_3), [near_3])
    out = None
    for units in ((0, 0), (0, 1)), ((1, 0), (1, 1)), ((2, 0), (2, 1)), ((4, 0), (4, 1)), ((3, 0), (5, 0)), ((3, 1), (5, 1)):
        out, after = ends(units, out, after)
    return out


def solution(mesh):
    wide, narrow = mesh.shape["wide"], mesh.shape["narrow"]

    def per_device(amplitudes, *others):
        fits = (wide, narrow) == (8, 4) and amplitudes.shape[0] == 12
        return (per_device_plane if fits else per_device_any)(amplitudes, *others)

    return jax.shard_map(
        per_device,
        mesh=mesh,
        in_specs=(
            P("narrow", None, "wide", None),
            P("narrow", None, "wide", None),
            P(None, None, None, "narrow"),
            P(None, None, "wide", "narrow"),
            P(),
            P(),
            P(),
            P(),
            P("narrow"),
            P(),
        ),
        out_specs=P("narrow", None, "wide", None),
        check_vma=False,
    )
```

```python
import functools

import jax
import jax.numpy as jnp
from jax import lax
from jax.experimental import pallas as pl
from jax.experimental.pallas import tpu as pltpu
from jax.sharding import PartitionSpec as P

VBLK = 16
CORE, XBIT, YBIT = 1, 2, 4
LANES = 512
VMEM = 60 * 2**20
COST = pl.CostEstimate(flops=0, bytes_accessed=1, transcendentals=0)


def spread(value, axis, source):
    kept = jnp.where(lax.axis_index(axis) == source, value, 0).astype(value.dtype)
    return lax.psum(kept, axis)


def lookup(indices, values_table):
    table_size = values_table.shape[0]
    matches = indices[:, None] == jnp.arange(table_size, dtype=jnp.int32)[None, :]
    return jnp.sum(
        jnp.where(matches, values_table[None, :], jnp.zeros_like(values_table)[None, :]), axis=1
    )


def cycle_product(amp_rows, weights):
    inner_k, inner_c, outer_j, outer_a = weights.shape
    flat_weights = weights.reshape(inner_k * inner_c, outer_j * outer_a)

    def one_row(amp_row):
        flat_row = amp_row.reshape(inner_k * inner_c, amp_row.shape[2])
        product = lax.dot_general(
            flat_weights, flat_row, (((0,), (0,)), ((), ())), preferred_element_type=jnp.float32
        )
        return product.reshape(outer_j, outer_a, amp_row.shape[2]).astype(jnp.bfloat16)

    return lax.map(one_row, amp_rows)


def per_device_any(
    amplitudes,
    pair_integrals,
    cycle_integrals,
    ladder_integrals,
    occ_energy,
    virt_energy,
    occ_irrep,
    virt_irrep,
    slab_i,
    slab_j,
):
    wide_count = lax.axis_size("wide")
    wide_index = lax.axis_index("wide")
    tile_width = ladder_integrals.shape[0]
    virt_count = virt_energy.shape[0]
    row_count = virt_count // wide_count
    relaid = lax.all_to_all(amplitudes, "wide", split_axis=3, concat_axis=2, tiled=True)
    tile_amps = spread(amplitudes[:, :, :tile_width, :], "wide", 0)
    ladder = jnp.einsum(
        "ijcd,acbd->ijab",
        tile_amps,
        lax.all_gather(ladder_integrals, "narrow", axis=3, tiled=True),
        preferred_element_type=jnp.float32,
    )
    cycle_local = cycle_product(
        relaid, lax.all_gather(cycle_integrals, "narrow", axis=3, tiled=True)
    )
    coupled_local = (
        cycle_local.astype(jnp.float32).at[:, :, :tile_width, :].add(ladder).astype(jnp.bfloat16)
    )
    coupled = lax.all_to_all(coupled_local, "wide", split_axis=2, concat_axis=3, tiled=True)
    energy_first = lookup(slab_i, occ_energy)
    energy_second = lookup(slab_j, occ_energy)
    label_first = lookup(slab_i, occ_irrep)
    label_second = lookup(slab_j, occ_irrep)
    label_virt = jnp.repeat(virt_irrep, VBLK)
    energy_rows = lax.dynamic_slice_in_dim(virt_energy, wide_index * row_count, row_count)
    label_rows = lax.dynamic_slice_in_dim(label_virt, wide_index * row_count, row_count)
    residual = pair_integrals.astype(jnp.float32) + coupled.astype(jnp.float32)
    denominator = (
        energy_rows[None, None, :, None]
        + virt_energy[None, None, None, :]
        - energy_first[:, None, None, None]
        - energy_second[None, :, None, None]
    )
    parity = (
        label_first[:, None, None, None]
        + label_second[None, :, None, None]
        + label_rows[None, None, :, None]
        + label_virt[None, None, None, :]
    ) % 2
    allowed = (1 - parity).astype(jnp.float32)
    return (allowed * residual / denominator).astype(jnp.bfloat16)


def cut_kernel(copies, passed, *refs):
    outs = refs[len(refs) - copies - passed :]
    for source, out in zip(refs[:copies], outs):
        out[...] = source[...]


def cut(amplitudes, pairs, handed_on, waited_for):
    anywhere = pl.BlockSpec(memory_space=pl.ANY)
    _, second, rows, cols = amplitudes.shape
    block = (2, 1, rows, cols)
    copies = len(pairs)
    outs = pl.pallas_call(
        functools.partial(cut_kernel, copies, len(handed_on)),
        grid=(second if copies else 1,),
        out_shape=(
            *(jax.ShapeDtypeStruct((2, second, rows, cols), amplitudes.dtype) for _ in pairs),
            *(jax.ShapeDtypeStruct(value.shape, value.dtype) for value in handed_on),
        ),
        in_specs=[
            *(pl.BlockSpec(block, lambda j, n=n: (n, j, 0, 0)) for n in pairs),
            *(anywhere for _ in [*handed_on, *waited_for]),
        ],
        out_specs=(
            *(pl.BlockSpec(block, lambda j: (0, j, 0, 0)) for _ in pairs),
            *(anywhere for _ in handed_on),
        ),
        input_output_aliases={copies + n: copies + n for n in range(len(handed_on))},
        compiler_params=pltpu.CompilerParams(vmem_limit_bytes=VMEM),
        cost_estimate=COST,
        name="cut",
    )(*[amplitudes] * copies, *handed_on, *waited_for)
    return outs[:copies], outs[copies:]


def blocks_kernel(place, weights, after, out_ref, handed, turned, picked):
    inner_k, row_count, outer_j, _ = weights.shape
    depth = inner_k * row_count
    flat = weights[...].reshape(depth * outer_j, weights.shape[3])
    mine = pl.ds(pl.multiple_of(place[1] * row_count, row_count), row_count)

    @pl.when(pl.program_id(0) == 0)
    def _():
        row = lax.broadcasted_iota(jnp.int32, picked.shape[1:], 0)
        col = lax.broadcasted_iota(jnp.int32, picked.shape[1:], 1)
        for j in range(outer_j):
            picked[j] = (row == outer_j * col + j).astype(picked.dtype)

    for j in range(outer_j):
        turned[...] = lax.dot_general(flat, picked[j], (((0,), (0,)), ((), ())), preferred_element_type=jnp.float32)
        out_ref[0, pl.ds(j * row_count, row_count), :] = turned[mine, :].astype(out_ref.dtype)


def weight_blocks(first, core, count, cycle_integrals, row_count, after):
    inner_k, _, outer_j, width = cycle_integrals.shape
    shape = (outer_j * row_count, inner_k * row_count)
    return pl.pallas_call(
        blocks_kernel,
        out_shape=(
            jax.ShapeDtypeStruct((count, *shape), cycle_integrals.dtype),
            jax.ShapeDtypeStruct(after.shape, after.dtype),
        ),
        grid_spec=pltpu.PrefetchScalarGridSpec(
            num_scalar_prefetch=1,
            grid=(count,),
            in_specs=[
                pl.BlockSpec((inner_k, row_count, outer_j, width), lambda n, s: (0, s[0] + n, 0, 0)),
                pl.BlockSpec(memory_space=pl.ANY),
            ],
            out_specs=(pl.BlockSpec((1, *shape), lambda n, s: (n, 0, 0)), pl.BlockSpec(memory_space=pl.ANY)),
            scratch_shapes=[
                pltpu.VMEM((width, shape[1]), jnp.float32),
                pltpu.VMEM((outer_j, shape[1] * outer_j, shape[1]), cycle_integrals.dtype),
            ],
        ),
        input_output_aliases={2: 1},
        compiler_params=pltpu.CompilerParams(vmem_limit_bytes=VMEM),
        cost_estimate=COST,
        name="weight_blocks",
    )(jnp.stack([first, core]).astype(jnp.int32), cycle_integrals, after)


def partial_kernel(sources, outs, scalars, *refs):
    blocks = len(set(sources))
    for_neighbour, for_self, refs = refs[:blocks], refs[blocks : 2 * blocks], refs[2 * blocks :]
    own, beside, near, far = refs[:4]
    *send, keep = refs[len(refs) - outs :]
    depth = own.shape[1] * own.shape[2]
    for unit in range(2):
        rows = [piece[unit].reshape(depth, piece.shape[3]) for piece in (own, beside, near, far)]
        rows = jnp.concatenate(rows, axis=0)
        to_send = send[0].at[unit] if len(send) == 1 else send[unit].at[0]
        for out, weights in ((to_send, for_neighbour), (keep.at[unit], for_self)):
            matrix = [weights[source][0, scalars[2 + n]] for n, source in enumerate(sources)]
            product = jnp.dot(jnp.concatenate(matrix, axis=1), rows, preferred_element_type=jnp.float32)
            out[...] = product.astype(out.dtype).reshape(out.shape)


def partial_sums(scalars, sources, weights, amplitudes, beside, near, far, pair, apart, waited_for):
    _, second, rows, cols = amplitudes.shape
    lanes = min(LANES, cols)
    out_rows, depth = weights[0].shape[2:]
    mine = pl.BlockSpec((2, second, rows, lanes), lambda n, s: (pair, 0, 0, n))
    both = pl.BlockSpec((2, second, rows, lanes), lambda n, s: (0, 0, 0, n))
    one = pl.BlockSpec((1, second, rows, lanes), lambda n, s: (0, 0, 0, n))
    for_neighbour = [pl.BlockSpec((1, *w.shape[1:]), lambda n, s: (s[0], 0, 0, 0)) for w in weights]
    for_self = [pl.BlockSpec((1, *w.shape[1:]), lambda n, s: (s[1], 0, 0, 0)) for w in weights]
    two = (2, second, rows, cols)
    send_shapes = [(1, *two[1:])] * 2 if apart else [two]
    outs = pl.pallas_call(
        functools.partial(partial_kernel, sources, len(send_shapes) + 1),
        out_shape=(
            *(jax.ShapeDtypeStruct(shape, jnp.bfloat16) for shape in send_shapes),
            jax.ShapeDtypeStruct(two, jnp.float32),
        ),
        grid_spec=pltpu.PrefetchScalarGridSpec(
            num_scalar_prefetch=1,
            grid=(cols // lanes,),
            in_specs=[
                *(*for_neighbour, *for_self, mine, mine, both, both),
                *(pl.BlockSpec(memory_space=pl.ANY) for _ in waited_for),
            ],
            out_specs=(*([one, one] if apart else [both]), both),
        ),
        compiler_params=pltpu.CompilerParams(vmem_limit_bytes=VMEM),
        cost_estimate=COST,
        name="partial_sums",
    )(scalars, *weights, *weights, amplitudes, beside, near, far, *waited_for)
    return outs[:-1], outs[-1]


def finish_kernel(indices, second_count, slab_i, slab_j, occ_energy, occ_irrep, *refs):
    units = len(indices)
    sums, refs = refs[: 2 * units], refs[2 * units :]
    pair, ladder, e_rows, l_rows, e_cols, l_cols = refs[:6]
    out_ref, token_ref, coupled = refs[-3:]
    second = pl.program_id(1)
    top = ladder.shape[0] // second_count
    for unit, index in enumerate(indices):
        keep, arrived = sums[2 * unit : 2 * unit + 2]

        @pl.when(pl.program_id(0) == unit)
        def _(index=index, keep=keep, arrived=arrived):
            cycle = (keep[0, 0] + arrived[0, 0].astype(jnp.float32)).astype(jnp.bfloat16)
            coupled[...] = cycle.astype(jnp.float32)
            mine = ladder[pl.ds(0, top), :]
            for j in range(1, ladder.shape[0] // top):
                mine = jnp.where(second == j, ladder[pl.ds(j * top, top), :], mine)
            with_ladder = coupled[pl.ds(0, top), :] + mine
            coupled[pl.ds(0, top), :] = with_ladder.astype(jnp.bfloat16).astype(jnp.float32)
            residual = pair[0, 0].astype(jnp.float32) + coupled[...]
            denominator = (e_rows[...] - occ_energy[slab_i[index]] - occ_energy[slab_j[second]]) + e_cols[...]
            odd_rows = (l_rows[...] + occ_irrep[slab_i[index]] + occ_irrep[slab_j[second]]) & 1
            value = jnp.where(odd_rows == l_cols[...] & 1, residual / denominator, 0.0)
            out_ref[0, 0] = value.astype(jnp.bfloat16)

    token_ref[...] = jnp.zeros_like(token_ref)


def finish(occupied, units, pair_integrals, ladder, virtual, so_far, after):
    _, second, rows, cols = pair_integrals.shape
    top = ladder.shape[0] // pair_integrals.shape[0]
    indices = tuple(index for index, *_ in units)
    step = indices[-1] - indices[0]
    block = (1, 1, rows, cols)
    at_index = pl.BlockSpec(block, lambda u, j, *s: (indices[0] + u * step, j, 0, 0))
    by_row = pl.BlockSpec((rows, 1), lambda u, j, *s: (0, 0))
    by_col = pl.BlockSpec((1, cols), lambda u, j, *s: (0, 0))
    operands, in_specs = [*occupied], []
    for unit, (_, *arrays) in enumerate(units):
        for array, place in arrays:
            own = lambda u, j, *s, unit=unit, place=place: (
                place,
                jnp.where(u == unit, j, jnp.where(u < unit, 0, second - 1)),
                0,
                0,
            )
            operands.append(array)
            in_specs.append(pl.BlockSpec(block, own))
    operands += [pair_integrals, ladder, *virtual]
    in_specs += [
        at_index,
        pl.BlockSpec((top, cols), lambda u, j, *s: (indices[0] + u * step, 0)),
        by_row,
        by_row,
        by_col,
        by_col,
    ]
    operands.append(after)
    in_specs.append(pl.BlockSpec(memory_space=pl.ANY))
    aliases = {}
    if so_far is not None:
        aliases = {len(operands): 0}
        operands.append(so_far)
        in_specs.append(pl.BlockSpec(memory_space=pl.ANY))
    return pl.pallas_call(
        functools.partial(finish_kernel, indices, second),
        out_shape=(
            jax.ShapeDtypeStruct(pair_integrals.shape, jnp.bfloat16),
            jax.ShapeDtypeStruct((8, 128), jnp.float32),
        ),
        grid_spec=pltpu.PrefetchScalarGridSpec(
            num_scalar_prefetch=4,
            grid=(len(units), second),
            in_specs=in_specs,
            out_specs=(at_index, pl.BlockSpec((8, 128), lambda u, j, *s: (0, 0))),
            scratch_shapes=[pltpu.VMEM((rows, cols), jnp.float32)],
        ),
        input_output_aliases=aliases,
        compiler_params=pltpu.CompilerParams(vmem_limit_bytes=VMEM),
        cost_estimate=COST,
        name="finish",
    )(*operands)


def per_device_plane(
    amplitudes,
    pair_integrals,
    cycle_integrals,
    ladder_integrals,
    occ_energy,
    virt_energy,
    occ_irrep,
    virt_irrep,
    slab_i,
    slab_j,
):
    wide_count, narrow_count = lax.axis_size("wide"), lax.axis_size("narrow")
    wide_index = lax.axis_index("wide")
    core, x, y = wide_index % 2, wide_index // 2 % 2, wide_index // 4
    count, second, row_count, virt_count = amplitudes.shape
    tile_width, _, _, ladder_depth = ladder_integrals.shape
    tile_rows = count * second * tile_width

    def across(value, bit):
        return lax.ppermute(value, "wide", [(w, w ^ bit) for w in range(wide_count)])

    tile = amplitudes[:, :, :tile_width, :].reshape(tile_rows, virt_count)
    near_blocks, tile = weight_blocks(4 * y, core, 4, cycle_integrals, row_count, tile)
    same_row = lax.all_gather(near_blocks, "narrow", axis=0)
    to_x, to_y, to_both = (lax.ppermute(tile, "wide", [(0, w)]) for w in (XBIT, YBIT, XBIT + YBIT))
    in_row = (x * 2 + core, x * 2 + 1 - core)
    numbers_x = jnp.stack(
        [2 * (1 - y) + x, 2 * y + x, *in_row, (1 - x) * 2 + core, (1 - x) * 2 + 1 - core]
    ).astype(jnp.int32)
    numbers_y = jnp.stack([2 * y + 1 - x, 2 * y + x, *in_row, core, 1 - core]).astype(jnp.int32)

    label_virt = jnp.repeat(virt_irrep, VBLK)
    energy_rows = lax.dynamic_slice_in_dim(virt_energy, wide_index * row_count, row_count)
    label_rows = lax.dynamic_slice_in_dim(label_virt, wide_index * row_count, row_count)
    occupied = (slab_i, slab_j, occ_energy, occ_irrep)
    virtual = (energy_rows[:, None], label_rows[:, None], virt_energy[None, :], label_virt[None, :])

    def ladder_amplitudes(to_x, to_y, to_both):
        corner = jnp.where(x == 0, jnp.where(y == 0, tile, to_y), jnp.where(y == 0, to_x, to_both))
        other = lax.ppermute(corner, "wide", [(w, w + CORE) for w in range(0, wide_count, 2)])
        every = jnp.where(core == 0, corner, other)
        every = every.reshape(tile_rows, narrow_count, ladder_depth).transpose(1, 0, 2)
        return lax.all_to_all(every, "narrow", split_axis=0, concat_axis=0, tiled=True)

    def ladder_product(every):
        every = every.reshape(-1, tile_width, ladder_depth)
        part = jnp.einsum("xcd,acbd->xab", every, ladder_integrals, preferred_element_type=jnp.float32)
        return part.astype(jnp.bfloat16).reshape(narrow_count, tile_rows, row_count)

    def ladder_chip(part):
        part = lax.all_to_all(part, "narrow", split_axis=0, concat_axis=0, tiled=True)
        part = part.astype(jnp.float32).sum(axis=0).astype(jnp.bfloat16)
        other = lax.ppermute(part, "wide", [(w + CORE, w) for w in range(0, wide_count, 2)])
        return jnp.concatenate([part, other], axis=1)

    along_x, along_y = (0, 1, 2, 3), (4, 5)
    kept, arrived = {}, {}

    def sums(pair, pieces, waited_for):
        plan = (numbers_x, (0, 0, 0, 0), (same_row,))
        if pair in along_y:
            plan = (numbers_y, (0, 0, 1, 1), (same_row, other_row))
        last = pair in (along_x[-1], along_y[-1])
        send, kept[pair] = partial_sums(*plan, amplitudes, beside, *pieces, pair, last, waited_for)
        there = [across(value, YBIT if pair in along_x else XBIT) for value in send]
        arrived[pair] = [(there[n], 0) if last else (there[0], n) for n in range(2)]
        return send[0]

    def ends(units, so_far, waited_for):
        units = [(2 * pair + n, (kept[pair], n), arrived[pair][n]) for pair, n in units]
        return finish(occupied, units, pair_integrals, ladder, virtual, so_far, waited_for)

    first, _ = cut(amplitudes, (0, 4), [], [near_blocks, to_x, to_y, to_both])
    beside = across(amplitudes, CORE)
    near_0, near_4 = across(first[0], XBIT), across(first[1], YBIT)
    then, to_all = cut(amplitudes, (1, 5), [to_x, to_y, to_both], [*first, beside])
    near_1, near_5 = across(then[0], XBIT), across(then[1], YBIT)
    tile_amps = ladder_amplitudes(*to_all)
    _, (near_0, near_4, tile_amps) = cut(amplitudes, (), [near_0, near_4, tile_amps], [*then, *virtual])
    far_0, far_4 = across(near_0, CORE), across(near_4, CORE)
    far_blocks, ladder_part = weight_blocks(
        4 * (1 - y) + 2 * x, core, 2, cycle_integrals, row_count, ladder_product(tile_amps)
    )
    other_row = lax.all_gather(far_blocks, "narrow", axis=0)
    chip_part = ladder_chip(ladder_part)
    third, _ = cut(amplitudes, (2,), [], [*then, far_0, far_4])
    near_2 = across(third[0], XBIT)
    after = sums(0, (near_0, far_0), [third[0], chip_part])
    from_x = lax.ppermute(chip_part, "wide", [(w + XBIT, w) for w in (0, YBIT)])
    _, (near_1, near_5, from_x) = cut(amplitudes, (), [near_1, near_5, from_x], [after])
    far_1, far_5 = across(near_1, CORE), across(near_5, CORE)
    row_part = jnp.concatenate([chip_part, from_x], axis=1)
    from_y = lax.ppermute(row_part, "wide", [(YBIT, 0)])
    fourth, _ = cut(amplitudes, (3,), [], [near_1, far_1, far_5])
    near_3 = across(fourth[0], XBIT)
    after = sums(1, (near_1, far_1), [fourth[0]])
    _, (near_2, from_y) = cut(amplitudes, (), [near_2, from_y], [after, arrived[0][0][0]])
    far_2 = across(near_2, CORE)
    after = sums(4, (near_4, far_4), [near_2])
    after = sums(2, (near_2, far_2), [after])
    after = sums(5, (near_5, far_5), [after])
    _, (near_3,) = cut(amplitudes, (), [near_3], [after, arrived[1][0][0]])
    far_3 = across(near_3, CORE)
    ladder = jnp.concatenate([row_part, from_y], axis=1).astype(jnp.float32)
    ladder = jnp.where(wide_index == 0, ladder, 0.0)
    after = sums(3, (near_3, far_3), [near_3])
    out = None
    for units in ((0, 0), (0, 1)), ((1, 0), (1, 1)), ((2, 0), (2, 1)), ((4, 0), (4, 1)), ((3, 0), (5, 0)), ((3, 1), (5, 1)):
        out, after = ends(units, out, after)
    return out


def solution(mesh):
    wide, narrow = mesh.shape["wide"], mesh.shape["narrow"]

    def per_device(amplitudes, *others):
        fits = (wide, narrow) == (8, 4) and amplitudes.shape[0] == 12
        return (per_device_plane if fits else per_device_any)(amplitudes, *others)

    return jax.shard_map(
        per_device,
        mesh=mesh,
        in_specs=(
            P("narrow", None, "wide", None),
            P("narrow", None, "wide", None),
            P(None, None, None, "narrow"),
            P(None, None, "wide", "narrow"),
            P(),
            P(),
            P(),
            P(),
            P("narrow"),
            P(),
        ),
        out_specs=P("narrow", None, "wide", None),
        check_vma=False,
    )
```

```python
import functools

import jax
import jax.numpy as jnp
from jax import lax
from jax.experimental import pallas as pl
from jax.experimental.pallas import tpu as pltpu
from jax.sharding import PartitionSpec as P

VBLK = 16
CORE, XBIT, YBIT = 1, 2, 4
LANES = 512
VMEM = 60 * 2**20
COST = pl.CostEstimate(flops=0, bytes_accessed=1, transcendentals=0)


def spread(value, axis, source):
    kept = jnp.where(lax.axis_index(axis) == source, value, 0).astype(value.dtype)
    return lax.psum(kept, axis)


def lookup(indices, values_table):
    table_size = values_table.shape[0]
    matches = indices[:, None] == jnp.arange(table_size, dtype=jnp.int32)[None, :]
    return jnp.sum(
        jnp.where(matches, values_table[None, :], jnp.zeros_like(values_table)[None, :]), axis=1
    )


def cycle_product(amp_rows, weights):
    inner_k, inner_c, outer_j, outer_a = weights.shape
    flat_weights = weights.reshape(inner_k * inner_c, outer_j * outer_a)

    def one_row(amp_row):
        flat_row = amp_row.reshape(inner_k * inner_c, amp_row.shape[2])
        product = lax.dot_general(
            flat_weights, flat_row, (((0,), (0,)), ((), ())), preferred_element_type=jnp.float32
        )
        return product.reshape(outer_j, outer_a, amp_row.shape[2]).astype(jnp.bfloat16)

    return lax.map(one_row, amp_rows)


def per_device_any(
    amplitudes,
    pair_integrals,
    cycle_integrals,
    ladder_integrals,
    occ_energy,
    virt_energy,
    occ_irrep,
    virt_irrep,
    slab_i,
    slab_j,
):
    wide_count = lax.axis_size("wide")
    wide_index = lax.axis_index("wide")
    tile_width = ladder_integrals.shape[0]
    virt_count = virt_energy.shape[0]
    row_count = virt_count // wide_count
    relaid = lax.all_to_all(amplitudes, "wide", split_axis=3, concat_axis=2, tiled=True)
    tile_amps = spread(amplitudes[:, :, :tile_width, :], "wide", 0)
    ladder = jnp.einsum(
        "ijcd,acbd->ijab",
        tile_amps,
        lax.all_gather(ladder_integrals, "narrow", axis=3, tiled=True),
        preferred_element_type=jnp.float32,
    )
    cycle_local = cycle_product(
        relaid, lax.all_gather(cycle_integrals, "narrow", axis=3, tiled=True)
    )
    coupled_local = (
        cycle_local.astype(jnp.float32).at[:, :, :tile_width, :].add(ladder).astype(jnp.bfloat16)
    )
    coupled = lax.all_to_all(coupled_local, "wide", split_axis=2, concat_axis=3, tiled=True)
    energy_first = lookup(slab_i, occ_energy)
    energy_second = lookup(slab_j, occ_energy)
    label_first = lookup(slab_i, occ_irrep)
    label_second = lookup(slab_j, occ_irrep)
    label_virt = jnp.repeat(virt_irrep, VBLK)
    energy_rows = lax.dynamic_slice_in_dim(virt_energy, wide_index * row_count, row_count)
    label_rows = lax.dynamic_slice_in_dim(label_virt, wide_index * row_count, row_count)
    residual = pair_integrals.astype(jnp.float32) + coupled.astype(jnp.float32)
    denominator = (
        energy_rows[None, None, :, None]
        + virt_energy[None, None, None, :]
        - energy_first[:, None, None, None]
        - energy_second[None, :, None, None]
    )
    parity = (
        label_first[:, None, None, None]
        + label_second[None, :, None, None]
        + label_rows[None, None, :, None]
        + label_virt[None, None, None, :]
    ) % 2
    allowed = (1 - parity).astype(jnp.float32)
    return (allowed * residual / denominator).astype(jnp.bfloat16)


def cut_kernel(copies, passed, *refs):
    outs = refs[len(refs) - copies - passed :]
    for source, out in zip(refs[:copies], outs):
        out[...] = source[...]


def cut(amplitudes, pairs, handed_on, waited_for):
    anywhere = pl.BlockSpec(memory_space=pl.ANY)
    _, second, rows, cols = amplitudes.shape
    block = (2, 1, rows, cols)
    copies = len(pairs)
    outs = pl.pallas_call(
        functools.partial(cut_kernel, copies, len(handed_on)),
        grid=(second if copies else 1,),
        out_shape=(
            *(jax.ShapeDtypeStruct((2, second, rows, cols), amplitudes.dtype) for _ in pairs),
            *(jax.ShapeDtypeStruct(value.shape, value.dtype) for value in handed_on),
        ),
        in_specs=[
            *(pl.BlockSpec(block, lambda j, n=n: (n, j, 0, 0)) for n in pairs),
            *(anywhere for _ in [*handed_on, *waited_for]),
        ],
        out_specs=(
            *(pl.BlockSpec(block, lambda j: (0, j, 0, 0)) for _ in pairs),
            *(anywhere for _ in handed_on),
        ),
        input_output_aliases={copies + n: copies + n for n in range(len(handed_on))},
        compiler_params=pltpu.CompilerParams(vmem_limit_bytes=VMEM),
        cost_estimate=COST,
        name="cut",
    )(*[amplitudes] * copies, *handed_on, *waited_for)
    return outs[:copies], outs[copies:]


def blocks_kernel(place, weights, after, out_ref, handed, turned, picked):
    inner_k, row_count, outer_j, _ = weights.shape
    depth = inner_k * row_count
    flat = weights[...].reshape(depth * outer_j, weights.shape[3])
    mine = pl.ds(pl.multiple_of(place[1] * row_count, row_count), row_count)

    @pl.when(pl.program_id(0) == 0)
    def _():
        row = lax.broadcasted_iota(jnp.int32, picked.shape[1:], 0)
        col = lax.broadcasted_iota(jnp.int32, picked.shape[1:], 1)
        for j in range(outer_j):
            picked[j] = (row == outer_j * col + j).astype(picked.dtype)

    for j in range(outer_j):
        turned[...] = lax.dot_general(flat, picked[j], (((0,), (0,)), ((), ())), preferred_element_type=jnp.float32)
        out_ref[0, pl.ds(j * row_count, row_count), :] = turned[mine, :].astype(out_ref.dtype)


def weight_blocks(first, core, count, cycle_integrals, row_count, after):
    inner_k, _, outer_j, width = cycle_integrals.shape
    shape = (outer_j * row_count, inner_k * row_count)
    return pl.pallas_call(
        blocks_kernel,
        out_shape=(
            jax.ShapeDtypeStruct((count, *shape), cycle_integrals.dtype),
            jax.ShapeDtypeStruct(after.shape, after.dtype),
        ),
        grid_spec=pltpu.PrefetchScalarGridSpec(
            num_scalar_prefetch=1,
            grid=(count,),
            in_specs=[
                pl.BlockSpec((inner_k, row_count, outer_j, width), lambda n, s: (0, s[0] + n, 0, 0)),
                pl.BlockSpec(memory_space=pl.ANY),
            ],
            out_specs=(pl.BlockSpec((1, *shape), lambda n, s: (n, 0, 0)), pl.BlockSpec(memory_space=pl.ANY)),
            scratch_shapes=[
                pltpu.VMEM((width, shape[1]), jnp.float32),
                pltpu.VMEM((outer_j, shape[1] * outer_j, shape[1]), cycle_integrals.dtype),
            ],
        ),
        input_output_aliases={2: 1},
        compiler_params=pltpu.CompilerParams(vmem_limit_bytes=VMEM),
        cost_estimate=COST,
        name="weight_blocks",
    )(jnp.stack([first, core]).astype(jnp.int32), cycle_integrals, after)


def partial_kernel(sources, outs, scalars, *refs):
    blocks = len(set(sources))
    for_neighbour, for_self, refs = refs[:blocks], refs[blocks : 2 * blocks], refs[2 * blocks :]
    own, beside, near, far = refs[:4]
    *send, keep = refs[len(refs) - outs :]
    depth = own.shape[1] * own.shape[2]
    for unit in range(2):
        rows = [piece[unit].reshape(depth, piece.shape[3]) for piece in (own, beside, near, far)]
        rows = jnp.concatenate(rows, axis=0)
        to_send = send[0].at[unit] if len(send) == 1 else send[unit].at[0]
        for out, weights in ((to_send, for_neighbour), (keep.at[unit], for_self)):
            matrix = [weights[source][0, scalars[2 + n]] for n, source in enumerate(sources)]
            product = jnp.dot(jnp.concatenate(matrix, axis=1), rows, preferred_element_type=jnp.float32)
            out[...] = product.astype(out.dtype).reshape(out.shape)


def partial_sums(scalars, sources, weights, amplitudes, beside, near, far, pair, apart, waited_for):
    _, second, rows, cols = amplitudes.shape
    lanes = min(LANES, cols)
    out_rows, depth = weights[0].shape[2:]
    mine = pl.BlockSpec((2, second, rows, lanes), lambda n, s: (pair, 0, 0, n))
    both = pl.BlockSpec((2, second, rows, lanes), lambda n, s: (0, 0, 0, n))
    one = pl.BlockSpec((1, second, rows, lanes), lambda n, s: (0, 0, 0, n))
    for_neighbour = [pl.BlockSpec((1, *w.shape[1:]), lambda n, s: (s[0], 0, 0, 0)) for w in weights]
    for_self = [pl.BlockSpec((1, *w.shape[1:]), lambda n, s: (s[1], 0, 0, 0)) for w in weights]
    two = (2, second, rows, cols)
    send_shapes = [(1, *two[1:])] * 2 if apart else [two]
    outs = pl.pallas_call(
        functools.partial(partial_kernel, sources, len(send_shapes) + 1),
        out_shape=(
            *(jax.ShapeDtypeStruct(shape, jnp.bfloat16) for shape in send_shapes),
            jax.ShapeDtypeStruct(two, jnp.float32),
        ),
        grid_spec=pltpu.PrefetchScalarGridSpec(
            num_scalar_prefetch=1,
            grid=(cols // lanes,),
            in_specs=[
                *(*for_neighbour, *for_self, mine, mine, both, both),
                *(pl.BlockSpec(memory_space=pl.ANY) for _ in waited_for),
            ],
            out_specs=(*([one, one] if apart else [both]), both),
        ),
        compiler_params=pltpu.CompilerParams(vmem_limit_bytes=VMEM),
        cost_estimate=COST,
        name="partial_sums",
    )(scalars, *weights, *weights, amplitudes, beside, near, far, *waited_for)
    return outs[:-1], outs[-1]


def finish_kernel(indices, second_count, slab_i, slab_j, occ_energy, occ_irrep, *refs):
    units = len(indices)
    sums, refs = refs[: 2 * units], refs[2 * units :]
    pair, ladder, e_rows, l_rows, e_cols, l_cols = refs[:6]
    out_ref, token_ref, coupled = refs[-3:]
    second = pl.program_id(1)
    top = ladder.shape[0] // second_count
    for unit, index in enumerate(indices):
        keep, arrived = sums[2 * unit : 2 * unit + 2]

        @pl.when(pl.program_id(0) == unit)
        def _(index=index, keep=keep, arrived=arrived):
            cycle = (keep[0, 0] + arrived[0, 0].astype(jnp.float32)).astype(jnp.bfloat16)
            coupled[...] = cycle.astype(jnp.float32)
            mine = ladder[pl.ds(0, top), :]
            for j in range(1, ladder.shape[0] // top):
                mine = jnp.where(second == j, ladder[pl.ds(j * top, top), :], mine)
            with_ladder = coupled[pl.ds(0, top), :] + mine
            coupled[pl.ds(0, top), :] = with_ladder.astype(jnp.bfloat16).astype(jnp.float32)
            residual = pair[0, 0].astype(jnp.float32) + coupled[...]
            denominator = (e_rows[...] - occ_energy[slab_i[index]] - occ_energy[slab_j[second]]) + e_cols[...]
            odd_rows = (l_rows[...] + occ_irrep[slab_i[index]] + occ_irrep[slab_j[second]]) & 1
            value = jnp.where(odd_rows == l_cols[...] & 1, residual / denominator, 0.0)
            out_ref[0, 0] = value.astype(jnp.bfloat16)

    token_ref[...] = jnp.zeros_like(token_ref)


def finish(occupied, units, pair_integrals, ladder, virtual, so_far, after):
    _, second, rows, cols = pair_integrals.shape
    top = ladder.shape[0] // pair_integrals.shape[0]
    indices = tuple(index for index, *_ in units)
    step = indices[-1] - indices[0]
    block = (1, 1, rows, cols)
    at_index = pl.BlockSpec(block, lambda u, j, *s: (indices[0] + u * step, j, 0, 0))
    by_row = pl.BlockSpec((rows, 1), lambda u, j, *s: (0, 0))
    by_col = pl.BlockSpec((1, cols), lambda u, j, *s: (0, 0))
    operands, in_specs = [*occupied], []
    for unit, (_, *arrays) in enumerate(units):
        for array, place in arrays:
            own = lambda u, j, *s, unit=unit, place=place: (
                place,
                jnp.where(u == unit, j, jnp.where(u < unit, 0, second - 1)),
                0,
                0,
            )
            operands.append(array)
            in_specs.append(pl.BlockSpec(block, own))
    operands += [pair_integrals, ladder, *virtual]
    in_specs += [
        at_index,
        pl.BlockSpec((top, cols), lambda u, j, *s: (indices[0] + u * step, 0)),
        by_row,
        by_row,
        by_col,
        by_col,
    ]
    operands.append(after)
    in_specs.append(pl.BlockSpec(memory_space=pl.ANY))
    aliases = {}
    if so_far is not None:
        aliases = {len(operands): 0}
        operands.append(so_far)
        in_specs.append(pl.BlockSpec(memory_space=pl.ANY))
    return pl.pallas_call(
        functools.partial(finish_kernel, indices, second),
        out_shape=(
            jax.ShapeDtypeStruct(pair_integrals.shape, jnp.bfloat16),
            jax.ShapeDtypeStruct((8, 128), jnp.float32),
        ),
        grid_spec=pltpu.PrefetchScalarGridSpec(
            num_scalar_prefetch=4,
            grid=(len(units), second),
            in_specs=in_specs,
            out_specs=(at_index, pl.BlockSpec((8, 128), lambda u, j, *s: (0, 0))),
            scratch_shapes=[pltpu.VMEM((rows, cols), jnp.float32)],
        ),
        input_output_aliases=aliases,
        compiler_params=pltpu.CompilerParams(vmem_limit_bytes=VMEM // 2),
        cost_estimate=COST,
        name="finish",
    )(*operands)


def per_device_plane(
    amplitudes,
    pair_integrals,
    cycle_integrals,
    ladder_integrals,
    occ_energy,
    virt_energy,
    occ_irrep,
    virt_irrep,
    slab_i,
    slab_j,
):
    wide_count, narrow_count = lax.axis_size("wide"), lax.axis_size("narrow")
    wide_index = lax.axis_index("wide")
    core, x, y = wide_index % 2, wide_index // 2 % 2, wide_index // 4
    count, second, row_count, virt_count = amplitudes.shape
    tile_width, _, _, ladder_depth = ladder_integrals.shape
    tile_rows = count * second * tile_width

    def across(value, bit):
        return lax.ppermute(value, "wide", [(w, w ^ bit) for w in range(wide_count)])

    tile = amplitudes[:, :, :tile_width, :].reshape(tile_rows, virt_count)
    near_blocks, tile = weight_blocks(4 * y, core, 4, cycle_integrals, row_count, tile)
    same_row = lax.all_gather(near_blocks, "narrow", axis=0)
    to_x, to_y, to_both = (lax.ppermute(tile, "wide", [(0, w)]) for w in (XBIT, YBIT, XBIT + YBIT))
    in_row = (x * 2 + core, x * 2 + 1 - core)
    numbers_x = jnp.stack(
        [2 * (1 - y) + x, 2 * y + x, *in_row, (1 - x) * 2 + core, (1 - x) * 2 + 1 - core]
    ).astype(jnp.int32)
    numbers_y = jnp.stack([2 * y + 1 - x, 2 * y + x, *in_row, core, 1 - core]).astype(jnp.int32)

    label_virt = jnp.repeat(virt_irrep, VBLK)
    energy_rows = lax.dynamic_slice_in_dim(virt_energy, wide_index * row_count, row_count)
    label_rows = lax.dynamic_slice_in_dim(label_virt, wide_index * row_count, row_count)
    occupied = (slab_i, slab_j, occ_energy, occ_irrep)
    virtual = (energy_rows[:, None], label_rows[:, None], virt_energy[None, :], label_virt[None, :])

    def ladder_amplitudes(to_x, to_y, to_both):
        corner = jnp.where(x == 0, jnp.where(y == 0, tile, to_y), jnp.where(y == 0, to_x, to_both))
        other = lax.ppermute(corner, "wide", [(w, w + CORE) for w in range(0, wide_count, 2)])
        every = jnp.where(core == 0, corner, other)
        every = every.reshape(tile_rows, narrow_count, ladder_depth).transpose(1, 0, 2)
        return lax.all_to_all(every, "narrow", split_axis=0, concat_axis=0, tiled=True)

    def ladder_product(every):
        every = every.reshape(-1, tile_width, ladder_depth)
        part = jnp.einsum("xcd,acbd->xab", every, ladder_integrals, preferred_element_type=jnp.float32)
        return part.astype(jnp.bfloat16).reshape(narrow_count, tile_rows, row_count)

    def ladder_chip(part):
        part = lax.all_to_all(part, "narrow", split_axis=0, concat_axis=0, tiled=True)
        part = part.astype(jnp.float32).sum(axis=0).astype(jnp.bfloat16)
        other = lax.ppermute(part, "wide", [(w + CORE, w) for w in range(0, wide_count, 2)])
        return jnp.concatenate([part, other], axis=1)

    along_x, along_y = (0, 1, 2, 3), (4, 5)
    kept, arrived = {}, {}

    def sums(pair, pieces, waited_for):
        plan = (numbers_x, (0, 0, 0, 0), (same_row,))
        if pair in along_y:
            plan = (numbers_y, (0, 0, 1, 1), (same_row, other_row))
        last = pair in (along_x[-1], along_y[-1])
        send, kept[pair] = partial_sums(*plan, amplitudes, beside, *pieces, pair, last, waited_for)
        there = [across(value, YBIT if pair in along_x else XBIT) for value in send]
        arrived[pair] = [(there[n], 0) if last else (there[0], n) for n in range(2)]
        return send[0]

    def ends(units, so_far, waited_for):
        units = [(2 * pair + n, (kept[pair], n), arrived[pair][n]) for pair, n in units]
        return finish(occupied, units, pair_integrals, ladder, virtual, so_far, waited_for)

    first, _ = cut(amplitudes, (0, 4), [], [near_blocks, to_x, to_y, to_both])
    beside = across(amplitudes, CORE)
    near_0, near_4 = across(first[0], XBIT), across(first[1], YBIT)
    then, to_all = cut(amplitudes, (1, 5), [to_x, to_y, to_both], [*first, beside])
    near_1, near_5 = across(then[0], XBIT), across(then[1], YBIT)
    tile_amps = ladder_amplitudes(*to_all)
    _, (near_0, near_4, tile_amps) = cut(amplitudes, (), [near_0, near_4, tile_amps], [*then, *virtual])
    far_0, far_4 = across(near_0, CORE), across(near_4, CORE)
    far_blocks, ladder_part = weight_blocks(
        4 * (1 - y) + 2 * x, core, 2, cycle_integrals, row_count, ladder_product(tile_amps)
    )
    other_row = lax.all_gather(far_blocks, "narrow", axis=0)
    chip_part = ladder_chip(ladder_part)
    third, _ = cut(amplitudes, (2,), [], [*then, far_0, far_4])
    near_2 = across(third[0], XBIT)
    after = sums(0, (near_0, far_0), [third[0], chip_part])
    from_x = lax.ppermute(chip_part, "wide", [(w + XBIT, w) for w in (0, YBIT)])
    _, (near_1, near_5, from_x) = cut(amplitudes, (), [near_1, near_5, from_x], [after])
    far_1, far_5 = across(near_1, CORE), across(near_5, CORE)
    row_part = jnp.concatenate([chip_part, from_x], axis=1)
    from_y = lax.ppermute(row_part, "wide", [(YBIT, 0)])
    fourth, _ = cut(amplitudes, (3,), [], [near_1, far_1, far_5])
    near_3 = across(fourth[0], XBIT)
    after = sums(1, (near_1, far_1), [fourth[0]])
    _, (near_2, from_y) = cut(amplitudes, (), [near_2, from_y], [after, arrived[0][0][0]])
    far_2 = across(near_2, CORE)
    after = sums(4, (near_4, far_4), [near_2])
    after = sums(2, (near_2, far_2), [after])
    after = sums(5, (near_5, far_5), [after])
    _, (near_3,) = cut(amplitudes, (), [near_3], [after, arrived[1][0][0]])
    far_3 = across(near_3, CORE)
    ladder = jnp.concatenate([row_part, from_y], axis=1).astype(jnp.float32)
    ladder = jnp.where(wide_index == 0, ladder, 0.0)
    after = sums(3, (near_3, far_3), [near_3])
    out = None
    for units in ((0, 0), (0, 1)), ((1, 0), (1, 1)), ((2, 0), (2, 1)), ((4, 0), (4, 1)), ((3, 0), (5, 0)), ((3, 1), (5, 1)):
        out, after = ends(units, out, after)
    return out


def solution(mesh):
    wide, narrow = mesh.shape["wide"], mesh.shape["narrow"]

    def per_device(amplitudes, *others):
        fits = (wide, narrow) == (8, 4) and amplitudes.shape[0] == 12
        return (per_device_plane if fits else per_device_any)(amplitudes, *others)

    return jax.shard_map(
        per_device,
        mesh=mesh,
        in_specs=(
            P("narrow", None, "wide", None),
            P("narrow", None, "wide", None),
            P(None, None, None, "narrow"),
            P(None, None, "wide", "narrow"),
            P(),
            P(),
            P(),
            P(),
            P("narrow"),
            P(),
        ),
        out_specs=P("narrow", None, "wide", None),
        check_vma=False,
    )
```

```python
import functools

import jax
import jax.numpy as jnp
from jax import lax
from jax.experimental import pallas as pl
from jax.experimental.pallas import tpu as pltpu
from jax.sharding import PartitionSpec as P

VBLK = 16
CORE, XBIT, YBIT = 1, 2, 4
LANES = 512
VMEM = 60 * 2**20
COST = pl.CostEstimate(flops=0, bytes_accessed=1, transcendentals=0)


def spread(value, axis, source):
    kept = jnp.where(lax.axis_index(axis) == source, value, 0).astype(value.dtype)
    return lax.psum(kept, axis)


def lookup(indices, values_table):
    table_size = values_table.shape[0]
    matches = indices[:, None] == jnp.arange(table_size, dtype=jnp.int32)[None, :]
    return jnp.sum(
        jnp.where(matches, values_table[None, :], jnp.zeros_like(values_table)[None, :]), axis=1
    )


def cycle_product(amp_rows, weights):
    inner_k, inner_c, outer_j, outer_a = weights.shape
    flat_weights = weights.reshape(inner_k * inner_c, outer_j * outer_a)

    def one_row(amp_row):
        flat_row = amp_row.reshape(inner_k * inner_c, amp_row.shape[2])
        product = lax.dot_general(
            flat_weights, flat_row, (((0,), (0,)), ((), ())), preferred_element_type=jnp.float32
        )
        return product.reshape(outer_j, outer_a, amp_row.shape[2]).astype(jnp.bfloat16)

    return lax.map(one_row, amp_rows)


def per_device_any(
    amplitudes,
    pair_integrals,
    cycle_integrals,
    ladder_integrals,
    occ_energy,
    virt_energy,
    occ_irrep,
    virt_irrep,
    slab_i,
    slab_j,
):
    wide_count = lax.axis_size("wide")
    wide_index = lax.axis_index("wide")
    tile_width = ladder_integrals.shape[0]
    virt_count = virt_energy.shape[0]
    row_count = virt_count // wide_count
    relaid = lax.all_to_all(amplitudes, "wide", split_axis=3, concat_axis=2, tiled=True)
    tile_amps = spread(amplitudes[:, :, :tile_width, :], "wide", 0)
    ladder = jnp.einsum(
        "ijcd,acbd->ijab",
        tile_amps,
        lax.all_gather(ladder_integrals, "narrow", axis=3, tiled=True),
        preferred_element_type=jnp.float32,
    )
    cycle_local = cycle_product(
        relaid, lax.all_gather(cycle_integrals, "narrow", axis=3, tiled=True)
    )
    coupled_local = (
        cycle_local.astype(jnp.float32).at[:, :, :tile_width, :].add(ladder).astype(jnp.bfloat16)
    )
    coupled = lax.all_to_all(coupled_local, "wide", split_axis=2, concat_axis=3, tiled=True)
    energy_first = lookup(slab_i, occ_energy)
    energy_second = lookup(slab_j, occ_energy)
    label_first = lookup(slab_i, occ_irrep)
    label_second = lookup(slab_j, occ_irrep)
    label_virt = jnp.repeat(virt_irrep, VBLK)
    energy_rows = lax.dynamic_slice_in_dim(virt_energy, wide_index * row_count, row_count)
    label_rows = lax.dynamic_slice_in_dim(label_virt, wide_index * row_count, row_count)
    residual = pair_integrals.astype(jnp.float32) + coupled.astype(jnp.float32)
    denominator = (
        energy_rows[None, None, :, None]
        + virt_energy[None, None, None, :]
        - energy_first[:, None, None, None]
        - energy_second[None, :, None, None]
    )
    parity = (
        label_first[:, None, None, None]
        + label_second[None, :, None, None]
        + label_rows[None, None, :, None]
        + label_virt[None, None, None, :]
    ) % 2
    allowed = (1 - parity).astype(jnp.float32)
    return (allowed * residual / denominator).astype(jnp.bfloat16)


def cut_kernel(copies, passed, *refs):
    outs = refs[len(refs) - copies - passed :]
    for source, out in zip(refs[:copies], outs):
        out[...] = source[...]


def cut(amplitudes, pairs, handed_on, waited_for):
    anywhere = pl.BlockSpec(memory_space=pl.ANY)
    _, second, rows, cols = amplitudes.shape
    block = (2, 1, rows, cols)
    copies = len(pairs)
    outs = pl.pallas_call(
        functools.partial(cut_kernel, copies, len(handed_on)),
        grid=(second if copies else 1,),
        out_shape=(
            *(jax.ShapeDtypeStruct((2, second, rows, cols), amplitudes.dtype) for _ in pairs),
            *(jax.ShapeDtypeStruct(value.shape, value.dtype) for value in handed_on),
        ),
        in_specs=[
            *(pl.BlockSpec(block, lambda j, n=n: (n, j, 0, 0)) for n in pairs),
            *(anywhere for _ in [*handed_on, *waited_for]),
        ],
        out_specs=(
            *(pl.BlockSpec(block, lambda j: (0, j, 0, 0)) for _ in pairs),
            *(anywhere for _ in handed_on),
        ),
        input_output_aliases={copies + n: copies + n for n in range(len(handed_on))},
        compiler_params=pltpu.CompilerParams(vmem_limit_bytes=VMEM),
        cost_estimate=COST,
        name="cut",
    )(*[amplitudes] * copies, *handed_on, *waited_for)
    return outs[:copies], outs[copies:]


def blocks_kernel(place, weights, after, out_ref, handed, turned, picked):
    inner_k, row_count, outer_j, _ = weights.shape
    depth = inner_k * row_count
    flat = weights[...].reshape(depth * outer_j, weights.shape[3])
    mine = pl.ds(pl.multiple_of(place[1] * row_count, row_count), row_count)

    @pl.when(pl.program_id(0) == 0)
    def _():
        row = lax.broadcasted_iota(jnp.int32, picked.shape[1:], 0)
        col = lax.broadcasted_iota(jnp.int32, picked.shape[1:], 1)
        for j in range(outer_j):
            picked[j] = (row == outer_j * col + j).astype(picked.dtype)

    for j in range(outer_j):
        turned[...] = lax.dot_general(flat, picked[j], (((0,), (0,)), ((), ())), preferred_element_type=jnp.float32)
        out_ref[0, pl.ds(j * row_count, row_count), :] = turned[mine, :].astype(out_ref.dtype)


def weight_blocks(first, core, count, cycle_integrals, row_count, after):
    inner_k, _, outer_j, width = cycle_integrals.shape
    shape = (outer_j * row_count, inner_k * row_count)
    return pl.pallas_call(
        blocks_kernel,
        out_shape=(
            jax.ShapeDtypeStruct((count, *shape), cycle_integrals.dtype),
            jax.ShapeDtypeStruct(after.shape, after.dtype),
        ),
        grid_spec=pltpu.PrefetchScalarGridSpec(
            num_scalar_prefetch=1,
            grid=(count,),
            in_specs=[
                pl.BlockSpec((inner_k, row_count, outer_j, width), lambda n, s: (0, s[0] + n, 0, 0)),
                pl.BlockSpec(memory_space=pl.ANY),
            ],
            out_specs=(pl.BlockSpec((1, *shape), lambda n, s: (n, 0, 0)), pl.BlockSpec(memory_space=pl.ANY)),
            scratch_shapes=[
                pltpu.VMEM((width, shape[1]), jnp.float32),
                pltpu.VMEM((outer_j, shape[1] * outer_j, shape[1]), cycle_integrals.dtype),
            ],
        ),
        input_output_aliases={2: 1},
        compiler_params=pltpu.CompilerParams(vmem_limit_bytes=VMEM),
        cost_estimate=COST,
        name="weight_blocks",
    )(jnp.stack([first, core]).astype(jnp.int32), cycle_integrals, after)


def partial_kernel(sources, outs, scalars, *refs):
    blocks = len(set(sources))
    for_neighbour, for_self, refs = refs[:blocks], refs[blocks : 2 * blocks], refs[2 * blocks :]
    own, beside, near, far = refs[:4]
    *send, keep = refs[len(refs) - outs :]
    depth = own.shape[1] * own.shape[2]
    for unit in range(2):
        rows = [piece[unit].reshape(depth, piece.shape[3]) for piece in (own, beside, near, far)]
        rows = jnp.concatenate(rows, axis=0)
        to_send = send[0].at[unit] if len(send) == 1 else send[unit].at[0]
        for out, weights in ((to_send, for_neighbour), (keep.at[unit], for_self)):
            matrix = [weights[source][0, scalars[2 + n]] for n, source in enumerate(sources)]
            product = jnp.dot(jnp.concatenate(matrix, axis=1), rows, preferred_element_type=jnp.float32)
            out[...] = product.astype(out.dtype).reshape(out.shape)


def partial_sums(scalars, sources, weights, amplitudes, beside, near, far, pair, apart, waited_for):
    _, second, rows, cols = amplitudes.shape
    lanes = min(LANES, cols)
    out_rows, depth = weights[0].shape[2:]
    mine = pl.BlockSpec((2, second, rows, lanes), lambda n, s: (pair, 0, 0, n))
    both = pl.BlockSpec((2, second, rows, lanes), lambda n, s: (0, 0, 0, n))
    one = pl.BlockSpec((1, second, rows, lanes), lambda n, s: (0, 0, 0, n))
    for_neighbour = [pl.BlockSpec((1, *w.shape[1:]), lambda n, s: (s[0], 0, 0, 0)) for w in weights]
    for_self = [pl.BlockSpec((1, *w.shape[1:]), lambda n, s: (s[1], 0, 0, 0)) for w in weights]
    two = (2, second, rows, cols)
    send_shapes = [(1, *two[1:])] * 2 if apart else [two]
    outs = pl.pallas_call(
        functools.partial(partial_kernel, sources, len(send_shapes) + 1),
        out_shape=(
            *(jax.ShapeDtypeStruct(shape, jnp.bfloat16) for shape in send_shapes),
            jax.ShapeDtypeStruct(two, jnp.float32),
        ),
        grid_spec=pltpu.PrefetchScalarGridSpec(
            num_scalar_prefetch=1,
            grid=(cols // lanes,),
            in_specs=[
                *(*for_neighbour, *for_self, mine, mine, both, both),
                *(pl.BlockSpec(memory_space=pl.ANY) for _ in waited_for),
            ],
            out_specs=(*([one, one] if apart else [both]), both),
        ),
        compiler_params=pltpu.CompilerParams(vmem_limit_bytes=VMEM),
        cost_estimate=COST,
        name="partial_sums",
    )(scalars, *weights, *weights, amplitudes, beside, near, far, *waited_for)
    return outs[:-1], outs[-1]


def finish_kernel(indices, second_count, slab_i, slab_j, occ_energy, occ_irrep, *refs):
    units = len(indices)
    sums, refs = refs[: 2 * units], refs[2 * units :]
    pair, ladder, e_rows, l_rows, e_cols, l_cols = refs[:6]
    out_ref, token_ref, coupled = refs[-3:]
    second = pl.program_id(1)
    top = ladder.shape[0] // second_count
    for unit, index in enumerate(indices):
        keep, arrived = sums[2 * unit : 2 * unit + 2]

        @pl.when(pl.program_id(0) == unit)
        def _(index=index, keep=keep, arrived=arrived):
            cycle = (keep[0, 0] + arrived[0, 0].astype(jnp.float32)).astype(jnp.bfloat16)
            coupled[...] = cycle.astype(jnp.float32)
            mine = ladder[pl.ds(0, top), :]
            for j in range(1, ladder.shape[0] // top):
                mine = jnp.where(second == j, ladder[pl.ds(j * top, top), :], mine)
            with_ladder = coupled[pl.ds(0, top), :] + mine
            coupled[pl.ds(0, top), :] = with_ladder.astype(jnp.bfloat16).astype(jnp.float32)
            residual = pair[0, 0].astype(jnp.float32) + coupled[...]
            denominator = (e_rows[...] - occ_energy[slab_i[index]] - occ_energy[slab_j[second]]) + e_cols[...]
            odd_rows = (l_rows[...] + occ_irrep[slab_i[index]] + occ_irrep[slab_j[second]]) & 1
            value = jnp.where(odd_rows == l_cols[...] & 1, residual / denominator, 0.0)
            out_ref[0, 0] = value.astype(jnp.bfloat16)

    token_ref[...] = jnp.zeros_like(token_ref)


def finish(occupied, units, pair_integrals, ladder, virtual, so_far, after):
    _, second, rows, cols = pair_integrals.shape
    top = ladder.shape[0] // pair_integrals.shape[0]
    indices = tuple(index for index, *_ in units)
    step = indices[-1] - indices[0]
    block = (1, 1, rows, cols)
    at_index = pl.BlockSpec(block, lambda u, j, *s: (indices[0] + u * step, j, 0, 0))
    by_row = pl.BlockSpec((rows, 1), lambda u, j, *s: (0, 0))
    by_col = pl.BlockSpec((1, cols), lambda u, j, *s: (0, 0))
    operands, in_specs = [*occupied], []
    for unit, (_, *arrays) in enumerate(units):
        for array, place in arrays:
            own = lambda u, j, *s, unit=unit, place=place: (
                place,
                jnp.where(u == unit, j, jnp.where(u < unit, 0, second - 1)),
                0,
                0,
            )
            operands.append(array)
            in_specs.append(pl.BlockSpec(block, own))
    operands += [pair_integrals, ladder, *virtual]
    in_specs += [
        at_index,
        pl.BlockSpec((top, cols), lambda u, j, *s: (indices[0] + u * step, 0)),
        by_row,
        by_row,
        by_col,
        by_col,
    ]
    operands.append(after)
    in_specs.append(pl.BlockSpec(memory_space=pl.ANY))
    aliases = {}
    if so_far is not None:
        aliases = {len(operands): 0}
        operands.append(so_far)
        in_specs.append(pl.BlockSpec(memory_space=pl.ANY))
    return pl.pallas_call(
        functools.partial(finish_kernel, indices, second),
        out_shape=(
            jax.ShapeDtypeStruct(pair_integrals.shape, jnp.bfloat16),
            jax.ShapeDtypeStruct((8, 128), jnp.float32),
        ),
        grid_spec=pltpu.PrefetchScalarGridSpec(
            num_scalar_prefetch=4,
            grid=(len(units), second),
            in_specs=in_specs,
            out_specs=(at_index, pl.BlockSpec((8, 128), lambda u, j, *s: (0, 0))),
            scratch_shapes=[pltpu.VMEM((rows, cols), jnp.float32)],
        ),
        input_output_aliases=aliases,
        compiler_params=pltpu.CompilerParams(vmem_limit_bytes=VMEM // 2),
        cost_estimate=COST,
        name="finish",
    )(*operands)


def per_device_plane(
    amplitudes,
    pair_integrals,
    cycle_integrals,
    ladder_integrals,
    occ_energy,
    virt_energy,
    occ_irrep,
    virt_irrep,
    slab_i,
    slab_j,
):
    wide_count, narrow_count = lax.axis_size("wide"), lax.axis_size("narrow")
    wide_index = lax.axis_index("wide")
    core, x, y = wide_index % 2, wide_index // 2 % 2, wide_index // 4
    count, second, row_count, virt_count = amplitudes.shape
    tile_width, _, _, ladder_depth = ladder_integrals.shape
    tile_rows = count * second * tile_width

    def across(value, bit):
        return lax.ppermute(value, "wide", [(w, w ^ bit) for w in range(wide_count)])

    tile = amplitudes[:, :, :tile_width, :].reshape(tile_rows, virt_count)
    near_blocks, tile = weight_blocks(4 * y, core, 4, cycle_integrals, row_count, tile)
    same_row = lax.all_gather(near_blocks, "narrow", axis=0)
    to_x, to_y, to_both = (lax.ppermute(tile, "wide", [(0, w)]) for w in (XBIT, YBIT, XBIT + YBIT))
    in_row = (x * 2 + core, x * 2 + 1 - core)
    numbers_x = jnp.stack(
        [2 * (1 - y) + x, 2 * y + x, *in_row, (1 - x) * 2 + core, (1 - x) * 2 + 1 - core]
    ).astype(jnp.int32)
    numbers_y = jnp.stack([2 * y + 1 - x, 2 * y + x, *in_row, core, 1 - core]).astype(jnp.int32)

    label_virt = jnp.repeat(virt_irrep, VBLK)
    energy_rows = lax.dynamic_slice_in_dim(virt_energy, wide_index * row_count, row_count)
    label_rows = lax.dynamic_slice_in_dim(label_virt, wide_index * row_count, row_count)
    occupied = (slab_i, slab_j, occ_energy, occ_irrep)
    virtual = (energy_rows[:, None], label_rows[:, None], virt_energy[None, :], label_virt[None, :])

    def ladder_amplitudes(to_x, to_y, to_both):
        corner = jnp.where(x == 0, jnp.where(y == 0, tile, to_y), jnp.where(y == 0, to_x, to_both))
        other = lax.ppermute(corner, "wide", [(w, w + CORE) for w in range(0, wide_count, 2)])
        every = jnp.where(core == 0, corner, other)
        every = every.reshape(tile_rows, narrow_count, ladder_depth).transpose(1, 0, 2)
        return lax.all_to_all(every, "narrow", split_axis=0, concat_axis=0, tiled=True)

    def ladder_product(every):
        every = every.reshape(-1, tile_width, ladder_depth)
        part = jnp.einsum("xcd,acbd->xab", every, ladder_integrals, preferred_element_type=jnp.float32)
        return part.astype(jnp.bfloat16).reshape(narrow_count, tile_rows, row_count)

    def ladder_chip(part):
        part = lax.all_to_all(part, "narrow", split_axis=0, concat_axis=0, tiled=True)
        part = part.astype(jnp.float32).sum(axis=0).astype(jnp.bfloat16)
        other = lax.ppermute(part, "wide", [(w + CORE, w) for w in range(0, wide_count, 2)])
        return jnp.concatenate([part, other], axis=1)

    along_x, along_y = (0, 1, 2, 3), (4, 5)
    kept, arrived = {}, {}

    def sums(pair, pieces, waited_for):
        plan = (numbers_x, (0, 0, 0, 0), (same_row,))
        if pair in along_y:
            plan = (numbers_y, (0, 0, 1, 1), (same_row, other_row))
        last = pair in (along_x[-1], along_y[-1])
        send, kept[pair] = partial_sums(*plan, amplitudes, beside, *pieces, pair, last, waited_for)
        there = [across(value, YBIT if pair in along_x else XBIT) for value in send]
        arrived[pair] = [(there[n], 0) if last else (there[0], n) for n in range(2)]
        return send[0]

    def ends(units, so_far, waited_for):
        units = [(2 * pair + n, (kept[pair], n), arrived[pair][n]) for pair, n in units]
        return finish(occupied, units, pair_integrals, ladder, virtual, so_far, waited_for)

    first, _ = cut(amplitudes, (0, 4), [], [near_blocks, to_x, to_y, to_both])
    beside = across(amplitudes, CORE)
    near_0, near_4 = across(first[0], XBIT), across(first[1], YBIT)
    then, to_all = cut(amplitudes, (1, 5), [to_x, to_y, to_both], [*first, beside])
    near_1, near_5 = across(then[0], XBIT), across(then[1], YBIT)
    tile_amps = ladder_amplitudes(*to_all)
    far_blocks, ladder_part = weight_blocks(
        4 * (1 - y) + 2 * x, core, 2, cycle_integrals, row_count, ladder_product(tile_amps)
    )
    other_row = lax.all_gather(far_blocks, "narrow", axis=0)
    chip_part = ladder_chip(ladder_part)
    _, (near_0, near_4) = cut(amplitudes, (), [near_0, near_4], [*then, *virtual, chip_part])
    far_0, far_4 = across(near_0, CORE), across(near_4, CORE)
    third, _ = cut(amplitudes, (2,), [], [*then, far_0, far_4])
    near_2 = across(third[0], XBIT)
    after = sums(0, (near_0, far_0), [third[0], chip_part])
    from_x = lax.ppermute(chip_part, "wide", [(w + XBIT, w) for w in (0, YBIT)])
    _, (near_1, near_5, from_x) = cut(amplitudes, (), [near_1, near_5, from_x], [after])
    far_1, far_5 = across(near_1, CORE), across(near_5, CORE)
    row_part = jnp.concatenate([chip_part, from_x], axis=1)
    from_y = lax.ppermute(row_part, "wide", [(YBIT, 0)])
    fourth, _ = cut(amplitudes, (3,), [], [near_1, far_1, far_5])
    near_3 = across(fourth[0], XBIT)
    after = sums(1, (near_1, far_1), [fourth[0]])
    _, (near_2, from_y) = cut(amplitudes, (), [near_2, from_y], [after, arrived[0][0][0]])
    far_2 = across(near_2, CORE)
    after = sums(4, (near_4, far_4), [near_2])
    after = sums(2, (near_2, far_2), [after])
    after = sums(5, (near_5, far_5), [after])
    _, (near_3,) = cut(amplitudes, (), [near_3], [after, arrived[1][0][0]])
    far_3 = across(near_3, CORE)
    ladder = jnp.concatenate([row_part, from_y], axis=1).astype(jnp.float32)
    ladder = jnp.where(wide_index == 0, ladder, 0.0)
    after = sums(3, (near_3, far_3), [near_3])
    out = None
    for units in ((0, 0), (0, 1)), ((1, 0), (1, 1)), ((2, 0), (2, 1)), ((4, 0), (4, 1)), ((3, 0), (5, 0)), ((3, 1), (5, 1)):
        out, after = ends(units, out, after)
    return out


def solution(mesh):
    wide, narrow = mesh.shape["wide"], mesh.shape["narrow"]

    def per_device(amplitudes, *others):
        fits = (wide, narrow) == (8, 4) and amplitudes.shape[0] == 12
        return (per_device_plane if fits else per_device_any)(amplitudes, *others)

    return jax.shard_map(
        per_device,
        mesh=mesh,
        in_specs=(
            P("narrow", None, "wide", None),
            P("narrow", None, "wide", None),
            P(None, None, None, "narrow"),
            P(None, None, "wide", "narrow"),
            P(),
            P(),
            P(),
            P(),
            P("narrow"),
            P(),
        ),
        out_specs=P("narrow", None, "wide", None),
        check_vma=False,
    )
```
